512 devices in a mesh: ta: 8 (over y), gx: 8 (over z_hi, core), gy: 8 (over x, z_lo).
Axes of the slice: x: 4, y: 8, z: 8 (z_hi: 4, z_lo: 2; z = z_hi * 2 + z_lo), core: 2. Of those that a mesh axis runs over, the one named last changes fastest.
Arguments:
- velocity: float32 [3, 8, 128, 128, 256], P(None, 'ta', 'gx', 'gy'), may hold values from -6 to 6
- pressure: float32 [8, 128, 128, 256], P('ta', 'gx', 'gy'), may hold values from -6 to 6
- forcing: float32 [3, 8, 128, 128, 256], P(None, 'ta', 'gx', 'gy'), may hold values from -6 to 6
- source: float32 [8, 128, 128, 256], P('ta', 'gx', 'gy'), may hold values from -6 to 6
- viscosity: float32 [3, 128, 128, 256], P(None, 'gx', 'gy'), may hold values from 0.05 to 0.5
Outputs:
- new_velocity: float32 [3, 8, 128, 128, 256], P(None, 'ta', 'gx', 'gy')
- new_pressure: float32 [8, 128, 128, 256], P('ta', 'gx', 'gy')
The draws below stay inside these ranges and needn't reach their ends.
All inputs are finite; a program needn't handle non-finite values.
Results may differ from the reference program's by a relative error of at most 0.00002.
Values sent between devices are 32-bit elements; how exact they have to be, the bound alone decides.
No kernel may reach another device: no remote copies, remote signals or barrier semaphores. Data moves between devices by JAX's collectives and lax.ppermute only.
A program may use at most 64 MiB of HBM per device.

```python
import math
import jax
import jax.numpy as jnp

CZ = 256
SWEEPS = 2
NT = 8
NX = 128
NY = 128


def levels(stream_key, dims, shards, least, largest):
    gain, own = 1.0, jax.random.fold_in(stream_key, 6)
    for position, parts in shards:
        draws = jnp.exp(jax.random.uniform(jax.random.fold_in(own, position), (parts,), jnp.float32, least / len(shards), largest / len(shards)))
        gain = gain * jnp.repeat(draws, dims[position] // parts).reshape([-1 if axis == position else 1 for axis in range(len(dims))])
    return gain


def bell_draw(own_key, dims, spread, most, split=(), held_as=jnp.bfloat16):
    result = spread * jax.random.normal(own_key, dims, jnp.float32)
    if split:
        result = result * levels(own_key, dims, split, -0.22, 0.18)
    return jnp.clip(result, -most, most).astype(held_as)


def setup_inputs(seed: int = 0) -> dict:
    seeds = jax.random.split(jax.random.key(seed), 6)
    velocity = bell_draw(seeds[0], (3, NT, NX, NY, CZ), 1.0, 6.0, ((1, 8), (2, 8), (3, 8)), jnp.float32)
    pressure = bell_draw(seeds[1], (NT, NX, NY, CZ), 1.0, 6.0, ((0, 8), (1, 8), (2, 8)), jnp.float32)
    forcing = bell_draw(seeds[2], (3, NT, NX, NY, CZ), 1.0, 6.0, ((1, 8), (2, 8), (3, 8)), jnp.float32)
    source = bell_draw(seeds[3], (NT, NX, NY, CZ), 1.0, 6.0, ((0, 8), (1, 8), (2, 8)), jnp.float32)
    viscosity = jnp.clip(jnp.exp(math.log(0.5) - 2.3025851 * jax.random.uniform(seeds[4], (3, NX, NY, CZ), jnp.float32) ** levels(seeds[4], (3, NX, NY, CZ), ((1, 8), (2, 8)), -0.2, 0.2)), 0.05, 0.5)
    return {"velocity": velocity, "pressure": pressure, "forcing": forcing, "source": source, "viscosity": viscosity}


inverse_step = 1.0
relax_factor = 1.5
damping = 0.8


def gradient(field):
    return jnp.stack([jnp.roll(field, -1, -3) - field, jnp.roll(field, -1, -2) - field, jnp.roll(field, -1, -1) - field])


def divergence(flux):
    return (flux[0] - jnp.roll(flux[0], 1, -3)) + (flux[1] - jnp.roll(flux[1], 1, -2)) + (flux[2] - jnp.roll(flux[2], 1, -1))


def neighbours(field):
    total = jnp.roll(field, 1, -3) + jnp.roll(field, -1, -3)
    total = total + jnp.roll(field, 1, -2) + jnp.roll(field, -1, -2)
    return total + jnp.roll(field, 1, -1) + jnp.roll(field, -1, -1)


def diagonal_sum(coeff):
    return coeff[0] + jnp.roll(coeff[0], 1, -3) + coeff[1] + jnp.roll(coeff[1], 1, -2) + coeff[2] + jnp.roll(coeff[2], 1, -1)


def reference(velocity, pressure, forcing, source, viscosity):
    previous = jnp.concatenate([jnp.zeros_like(velocity[:, :1]), velocity[:, :-1]], axis=1)
    driven = forcing + inverse_step * previous
    visc = viscosity[:, None]
    momentum = driven - (inverse_step * velocity + visc * (6.0 * velocity - neighbours(velocity))) - gradient(pressure)
    coeff = 1.0 / (relax_factor * (inverse_step + 6.0 * visc))
    total = diagonal_sum(coeff)
    right = divergence(coeff * momentum) - (source - divergence(velocity))
    change = -damping * right / total
    for sweep in range(SWEEPS - 1):
        change = change - damping * (right - divergence(coeff * gradient(change))) / total
    new_velocity = velocity + coeff * (momentum - gradient(change))
    return new_velocity, pressure + change
```

```python
import functools

import jax
import jax.numpy as jnp
from jax import lax
from jax.experimental import pallas as pl
from jax.experimental.pallas import tpu as pltpu
from jax.sharding import PartitionSpec as P

RELAX = 1.5
DAMPING = 0.8
EXT = 24


def odd_pairs(n):
    return [p for i in range(1, n, 2) for p in ((i, (i + 1) % n), ((i + 1) % n, i))]


def even_pairs(n):
    return [p for i in range(0, n, 2) for p in ((i, i + 1), (i + 1, i))]


def swap_odd(x, axis):
    return lax.ppermute(x, axis, odd_pairs(lax.axis_size(axis)))


def swap_even(x, axis):
    return lax.ppermute(x, axis, even_pairs(lax.axis_size(axis)))


def above_z(x):
    return pltpu.roll(x, x.shape[1] - 1, 1)


def below_z(x):
    return pltpu.roll(x, 1, 1)


def above_y(x):
    return pltpu.roll(x, x.shape[0] - 1, 0)


def below_y(x):
    return pltpu.roll(x, 1, 0)


def row_id(shape):
    return lax.broadcasted_iota(jnp.int32, shape, 0)


def coeff_of(visc):
    return 1.0 / (RELAX * (1.0 + 6.0 * visc))


def local_kernel(v, p, f, visc, flux, coeff):
    nx, ny = p.shape[0], p.shape[1]
    rows = row_id(p.shape[1:])
    first, last = rows == 0, rows == ny - 1
    for i in range(nx):
        pressure = p[i]
        slope_x = (p[i + 1] if i + 1 < nx else jnp.zeros_like(pressure)) - pressure
        slope_y = jnp.where(last, 0.0, above_y(pressure)) - pressure
        slope_z = above_z(pressure) - pressure
        for c, slope in enumerate((slope_x, slope_y, slope_z)):
            nu = visc[c, i]
            k = coeff_of(nu)
            flow = v[c, i]
            near = above_z(flow) + below_z(flow)
            near = near + jnp.where(last, 0.0, above_y(flow)) + jnp.where(first, 0.0, below_y(flow))
            if i > 0:
                near = near + v[c, i - 1]
            if i + 1 < nx:
                near = near + v[c, i + 1]
            coeff[c, i] = k
            flux[c, i] = k * (f[c, i] + nu * near - slope) + flow * (1.0 - 1.0 / RELAX)


def edge_kernel(
    parity, flux0, coeff, prev, s, v_lo_x, v_hi_x, v_lo_y, v_hi_y,
    flux, part, scale, send_odd, send_even,
):
    nx, ny = s.shape[0], s.shape[1]
    shape = s.shape[1:]
    rows = row_id(shape)
    first, last = rows == 0, rows == ny - 1
    even_y = parity[1] == 0
    zero = jnp.zeros((1, shape[1]), jnp.float32)

    def send(layer, i, up, down):
        send_even[layer, i : i + 1, :] = jnp.where(even_y, up, down)
        send_odd[layer, i : i + 1, :] = jnp.where(even_y, down, up)

    for i in range(nx):
        own = []
        for c in range(3):
            k = coeff[c, i]
            a = (1.0 / RELAX - k) * (1.0 / 6.0)
            near = jnp.where(first, v_lo_y[c, i : i + 1, :], 0.0)
            near = near + jnp.where(last, v_hi_y[c, i : i + 1, :], 0.0)
            if i == 0:
                near = near + v_lo_x[c]
            if i == nx - 1:
                near = near + v_hi_x[c]
            value = flux0[c, i] + k * prev[c, i] + a * near
            if c == 0 and i == nx - 1:
                value = value - k * v_hi_x[3]
            if c == 1:
                value = value - k * jnp.where(last, v_hi_y[3, i : i + 1, :], 0.0)
            flux[c, i] = value
            own.append(value)
        right = own[0] + own[1] - jnp.where(first, 0.0, below_y(own[1])) + own[2] - below_z(own[2])
        right = right - s[i]
        kx, ky, kz = coeff[0, i], coeff[1, i], coeff[2, i]
        total = kx + ky + jnp.where(first, v_lo_y[3, i : i + 1, :], below_y(ky)) + kz + below_z(kz)
        if i > 0:
            right = right - flux[0, i - 1]
            total = total + coeff[0, i - 1]
        else:
            total = total + v_lo_x[3]
        over = -DAMPING / total
        part[i] = right
        scale[i] = over
        send(0, i, right[ny - 1 :, :], right[:1, :])
        send(1, i, own[1][ny - 1 :, :], right[1:2, :])
        send(2, i, over[ny - 1 :, :], over[:1, :])
        send(3, i, zero, over[1:2, :])
        if i == nx - 1:
            send(4, 0, own[0][ny - 1 :, :], own[0][:1, :])
            send(4, 1, zero, own[0][1:2, :])
            for j in range(2, nx):
                send(4, j, zero, zero)


def pick(even, odd_got, even_got, index):
    a, b = odd_got[index], even_got[index]
    return jnp.where(even, a, b), jnp.where(even, b, a)


def extend(dst, index, own, r16, r17, low):
    n = own.shape[0]
    dst[index, 0:n, :] = own
    dst[index, n : n + 1, :] = r16
    dst[index, n + 1 : n + 2, :] = r17
    dst[index, EXT - 1 : EXT, :] = low


def joined(i, even_y, got_odd, got_even, part, flux, right_x, scale_x, scale, index):
    ny = part.shape[1]
    row = slice(i, i + 1)
    lo0, hi0 = pick(even_y, got_odd, got_even, (0, row))
    lo1, hi1 = pick(even_y, got_odd, got_even, (1, row))
    lo2, hi2 = pick(even_y, got_odd, got_even, (2, row))
    _, hi3 = pick(even_y, got_odd, got_even, (3, row))
    own = part[i]
    own = own - jnp.where(row_id(own.shape) == 0, lo1, 0.0)
    extend(right_x, index, own, hi0 - flux[1, i, ny - 1 : ny, :], hi1, lo0)
    extend(scale_x, index, scale[i], hi2, hi3, lo2)


def side_strip(dst, index, even_y, got_odd, got_even, flux):
    nx = flux.shape[1]
    lo, hi = pick(even_y, got_odd, got_even, (4, slice(0, 1)))
    _, hi1 = pick(even_y, got_odd, got_even, (4, slice(1, 2)))
    extend(dst, index, flux[0, nx - 1], hi, hi1, lo)


def strip_kernel(
    parity, flux, part, scale, coeff, lo_y, hi_y, got_odd, got_even,
    send_odd, send_even, right_x, scale_x, side,
):
    nx, ny = part.shape[0], part.shape[1]
    even_x, even_y = parity[0] == 0, parity[1] == 0
    right_x[...] = jnp.zeros_like(right_x)
    scale_x[...] = jnp.zeros_like(scale_x)
    side[...] = jnp.zeros_like(side)
    for n, i in enumerate((0, 1, nx - 1)):
        joined(i, even_y, got_odd, got_even, part, flux, right_x, scale_x, scale, n)
    side_strip(side, 0, even_y, got_odd, got_even, flux)
    side[0, ny + 2 : ny + 3, :] = hi_y[4, nx - 1 : nx, :]
    scale_x[0, ny + 2 : ny + 3, :] = lo_y[3, 0:1, :]

    def send(layer, up, down):
        send_even[layer] = jnp.where(even_x, up, down)
        send_odd[layer] = jnp.where(even_x, down, up)

    send(0, right_x[2] * scale_x[2], right_x[1] * scale_x[1])
    send(1, side[0], right_x[0])
    send(2, jnp.zeros(side.shape[1:], jnp.float32), scale_x[0])


def last_kernel(
    parity, flux, part, scale, coeff, p, lo_x, hi_x, lo_y, hi_y,
    got_odd_y, got_even_y, got_odd_x, got_even_x,
    new_v, new_p, right_x, scale_x, side, first_c, kx, ky, kz,
):
    nx, ny = part.shape[0], part.shape[1]
    even_x, even_y = parity[0] == 0, parity[1] == 0
    right_x[...] = jnp.zeros_like(right_x)
    scale_x[...] = jnp.zeros_like(scale_x)
    lo0, hi0 = pick(even_x, got_odd_x, got_even_x, 0)
    lo1, hi1 = pick(even_x, got_odd_x, got_even_x, 1)
    _, hi2 = pick(even_x, got_odd_x, got_even_x, 2)
    side[...] = jnp.zeros_like(side)
    side_strip(side, 0, even_y, got_odd_y, got_even_y, flux)
    first_c[0] = lo0
    for i in range(nx):
        joined(i, even_y, got_odd_y, got_even_y, part, flux, right_x, scale_x, scale, i)
        right = right_x[i]
        if i == 0:
            right = right - lo1
        first_c[i + 1] = right * scale_x[i]
    first_c[nx + 1] = (hi1 - side[0]) * hi2
    first_c[nx + 2] = hi0
    scale_x[nx] = hi2
    zero = jnp.zeros((1, part.shape[2]), jnp.float32)
    extend(kx, 0, lo_x[3], lo1[ny + 2 : ny + 3, :], zero, zero)
    for i in range(nx):
        row = slice(i, i + 1)
        extend(kx, i + 1, coeff[0, i], hi_y[4, row, :], zero, zero)
        extend(ky, i, coeff[1, i], hi_y[5, row, :], zero, lo_y[3, row, :])
        extend(kz, i, coeff[2, i], hi_y[6, row, :], zero, zero)
    extend(kx, nx + 1, hi_x[4], zero, zero, zero)
    extend(ky, nx, hi_x[5], zero, zero, hi2[ny + 2 : ny + 3, :])
    extend(kz, nx, hi_x[6], zero, zero, zero)

    def sweep(i):
        mid = first_c[i + 1]
        gx = kx[i + 1] * (first_c[i + 2] - mid) - kx[i] * (mid - first_c[i])
        gy = ky[i] * (above_y(mid) - mid)
        gz = kz[i] * (above_z(mid) - mid)
        applied = gx + gy - below_y(gy) + gz - below_z(gz)
        return 2.0 * mid - scale_x[i] * applied

    now = sweep(0)
    for i in range(nx):
        after = sweep(i + 1)
        new_p[i] = p[i] + now[:ny]
        new_v[0, i] = flux[0, i] - coeff[0, i] * (after - now)[:ny]
        new_v[1, i] = flux[1, i] - coeff[1, i] * (above_y(now) - now)[:ny]
        new_v[2, i] = flux[2, i] - coeff[2, i] * (above_z(now) - now)[:ny]
        now = after


VM = pl.BlockSpec(memory_space=pltpu.VMEM)
SM = pl.BlockSpec(memory_space=pltpu.SMEM)


def call(kernel, args, outs, scratch=(), scalars=True):
    shapes = [jax.ShapeDtypeStruct(s, jnp.float32) for s in outs]
    size = sum(4 * a.size for a in args) + sum(4 * s.size for s in shapes)
    specs = [SM] + [VM] * (len(args) - 1) if scalars else [VM] * len(args)
    return pl.pallas_call(
        kernel,
        out_shape=shapes,
        in_specs=specs,
        out_specs=[VM] * len(shapes),
        scratch_shapes=[pltpu.VMEM(s, jnp.float32) for s in scratch],
        compiler_params=pltpu.CompilerParams(vmem_limit_bytes=40 * 2**20),
        cost_estimate=pl.CostEstimate(flops=size * 4, bytes_accessed=size, transcendentals=0),
    )(*args)


def faces(v, p, visc, dim):
    size = p.shape[dim]
    low = lambda x, d: lax.index_in_dim(x, 0, d, keepdims=False)
    top = lambda x, d: lax.index_in_dim(x, size - 1, d, keepdims=False)
    up = jnp.concatenate([top(v, dim + 1), coeff_of(top(visc[dim], dim))[None]], 0)
    up = jnp.concatenate([up, jnp.zeros((3,) + up.shape[1:], up.dtype)], 0)
    down = jnp.concatenate([low(v, dim + 1), low(p, dim)[None], coeff_of(low(visc, dim + 1))], 0)
    return up, down


def exchange(up, down, axis, even):
    odd_got = swap_odd(jnp.where(even, down, up), axis)
    even_got = swap_even(jnp.where(even, up, down), axis)
    return jnp.where(even, odd_got, even_got), jnp.where(even, even_got, odd_got)


def body(velocity, pressure, forcing, source, viscosity):
    v, p, f, s = velocity[:, 0], pressure[0], forcing[:, 0], source[0]
    nx, ny, nz = p.shape
    steps = lax.axis_size("ta")
    prev = lax.ppermute(v, "ta", [(i, i + 1) for i in range(steps - 1)])
    parity = jnp.stack([lax.axis_index("gx") % 2, lax.axis_index("gy") % 2]).astype(jnp.int32)
    even_x, even_y = parity[0] == 0, parity[1] == 0
    lo_y, hi_y = exchange(*faces(v, p, viscosity, 1), "gy", even_y)
    lo_x, hi_x = exchange(*faces(v, p, viscosity, 0), "gx", even_x)
    flux0, coeff = call(local_kernel, (v, p, f, viscosity), (v.shape, v.shape), scalars=False)
    flux, part, scale, send_odd, send_even = call(
        edge_kernel,
        (parity, flux0, coeff, prev, s, lo_x, hi_x, lo_y, hi_y),
        (v.shape, p.shape, p.shape, (5, nx, nz), (5, nx, nz)),
    )
    odd_y, even_y_got = swap_odd(send_odd, "gy"), swap_even(send_even, "gy")
    send_odd, send_even = call(
        strip_kernel,
        (parity, flux, part, scale, coeff, lo_y, hi_y, odd_y, even_y_got),
        ((3, EXT, nz), (3, EXT, nz)),
        ((3, EXT, nz), (3, EXT, nz), (1, EXT, nz)),
    )
    odd_x, even_x_got = swap_odd(send_odd, "gx"), swap_even(send_even, "gx")
    new_v, new_p = call(
        last_kernel,
        (parity, flux, part, scale, coeff, p, lo_x, hi_x, lo_y, hi_y, odd_y, even_y_got, odd_x, even_x_got),
        (v.shape, p.shape),
        (
            (nx, EXT, nz), (nx + 1, EXT, nz), (1, EXT, nz), (nx + 3, EXT, nz),
            (nx + 2, EXT, nz), (nx + 1, EXT, nz), (nx + 1, EXT, nz),
        ),
    )
    return new_v[:, None], new_p[None]


def solution(mesh):
    placed = (
        P(None, "ta", "gx", "gy", None),
        P("ta", "gx", "gy", None),
        P(None, "ta", "gx", "gy", None),
        P("ta", "gx", "gy", None),
        P(None, "gx", "gy", None),
    )
    return jax.shard_map(
        body,
        mesh=mesh,
        in_specs=placed,
        out_specs=(P(None, "ta", "gx", "gy", None), P("ta", "gx", "gy", None)),
        check_vma=False,
    )
```

```python
import jax
import jax.numpy as jnp
from jax import lax
from jax.experimental import pallas as pl
from jax.experimental.pallas import tpu as pltpu
from jax.sharding import PartitionSpec as P

RELAX = 1.5
DAMPING = 0.8
EXT = 24


def odd_pairs(n):
    return [p for i in range(1, n, 2) for p in ((i, (i + 1) % n), ((i + 1) % n, i))]


def even_pairs(n):
    return [p for i in range(0, n, 2) for p in ((i, i + 1), (i + 1, i))]


def swap_odd(x, axis):
    return lax.ppermute(x, axis, odd_pairs(lax.axis_size(axis)))


def swap_even(x, axis):
    return lax.ppermute(x, axis, even_pairs(lax.axis_size(axis)))


def above_z(x):
    return pltpu.roll(x, x.shape[1] - 1, 1)


def below_z(x):
    return pltpu.roll(x, 1, 1)


def above_y(x):
    return pltpu.roll(x, x.shape[0] - 1, 0)


def below_y(x):
    return pltpu.roll(x, 1, 0)


def row_id(shape):
    return lax.broadcasted_iota(jnp.int32, shape, 0)


def coeff_of(visc):
    return 1.0 / (RELAX * (1.0 + 6.0 * visc))


def ring_plan(nx, ny):
    layers = [(c, i) for c in range(3) for i in (0, 1, nx - 1)] + [(0, nx - 2)]
    whole = {key: tile for tile, key in enumerate(layers)}
    lines = [(0, 1, ny - 1), (0, 1, ny - 2, ny - 1), (0, 1, ny - 1)]
    single = {}
    for c in range(3):
        for i in range(nx):
            if (c, i) not in whole:
                for j in lines[c]:
                    tile, row = divmod(len(single), ny)
                    single[c, i, j] = (len(whole) + tile, row)
    return whole, single, lines, len(whole) + -(-len(single) // ny)


def share(c):
    return (1.0 / RELAX - c) * (1.0 / 6.0)


def pick(even, odd_got, even_got, index):
    a, b = odd_got[index], even_got[index]
    return jnp.where(even, a, b), jnp.where(even, b, a)


def ring_kernel(v, ring):
    nx, ny = v.shape[1], v.shape[2]
    whole, single, _, tiles = ring_plan(nx, ny)
    ring[tiles - 1] = jnp.zeros(ring.shape[1:], jnp.float32)
    for (c, i), tile in whole.items():
        ring[tile] = v[c, i]
    for (c, i, j), (tile, row) in single.items():
        ring[tile, row : row + 1, :] = v[c, i, j : j + 1, :]


def face_kernel(parity, v, p, visc, send_odd, send_even):
    nx = v.shape[1]
    even_x = parity[0] == 0

    def send(layer, up, down):
        send_even[layer] = jnp.where(even_x, up, down)
        send_odd[layer] = jnp.where(even_x, down, up)

    for c in range(3):
        send(c, v[c, nx - 1], v[c, 0])
        send(4 + c, coeff_of(visc[c, nx - 1]), coeff_of(visc[c, 0]))
    send(3, jnp.zeros(p.shape[1:], jnp.float32), p[0])


def local_kernel(v, p, f, visc, ring, flux, coeff):
    nx, ny = p.shape[0], p.shape[1]
    rows = row_id(p.shape[1:])
    first, last = rows == 0, rows == ny - 1
    whole, single, lines, _ = ring_plan(nx, ny)
    for i in range(nx):
        pressure = p[i]
        slope_x = (p[i + 1] if i + 1 < nx else jnp.zeros_like(pressure)) - pressure
        slope_y = jnp.where(last, 0.0, above_y(pressure)) - pressure
        slope_z = above_z(pressure) - pressure
        for c, slope in enumerate((slope_x, slope_y, slope_z)):
            nu = visc[c, i]
            k = coeff_of(nu)
            flow = v[c, i]
            near = above_z(flow) + below_z(flow)
            near = near + jnp.where(last, 0.0, above_y(flow)) + jnp.where(first, 0.0, below_y(flow))
            if i > 0:
                near = near + v[c, i - 1]
            if i + 1 < nx:
                near = near + v[c, i + 1]
            coeff[c, i] = k
            if (c, i) in whole:
                prev = ring[whole[c, i]]
            else:
                prev = jnp.zeros(p.shape[1:], jnp.float32)
                for j in lines[c]:
                    tile, row = single[c, i, j]
                    prev = jnp.where(rows == j, ring[tile, row : row + 1, :], prev)
            flux[c, i] = k * (f[c, i] + prev + nu * near - slope) + flow * (1.0 - 1.0 / RELAX)


def edge_kernel(parity, flux0, coeff, v, p, s, got_odd, got_even, lo_x, hi_x, total, send_odd, send_even, own, inner):
    nx, ny = s.shape[0], s.shape[1]
    shape = s.shape[1:]
    rows = row_id(shape)
    first = rows == 0
    even_y = parity[1] == 0
    zero = jnp.zeros((1, shape[1]), jnp.float32)
    top, low, near = slice(ny - 1, ny), slice(0, 1), slice(1, 2)
    for layer in range(7):
        lo_x[layer], hi_x[layer] = pick(parity[0] == 0, got_odd, got_even, layer)

    def send(layer, i, up, down):
        send_even[layer, i : i + 1, :] = jnp.where(even_y, up, down)
        send_odd[layer, i : i + 1, :] = jnp.where(even_y, down, up)

    before = None
    for i in range(nx):
        row = slice(i, i + 1)
        flows = []
        for c in range(3):
            if 1 < i < nx - 1:
                inner[c, i - 2] = v[c, i]
            k = coeff[c, i]
            value = flux0[c, i]
            if i == 0:
                value = value + share(k) * lo_x[c]
            if i == nx - 1:
                value = value + share(k) * hi_x[c]
                if c == 0:
                    value = value - k * hi_x[3]
            flows.append(value)
        right = flows[0] + flows[1] - jnp.where(first, 0.0, below_y(flows[1])) + flows[2] - below_z(flows[2])
        right = right - s[i]
        kx, ky, kz = coeff[0, i], coeff[1, i], coeff[2, i]
        tot = kx + ky + jnp.where(first, 0.0, below_y(ky)) + kz + below_z(kz)
        if i > 0:
            right = right - before
            tot = tot + coeff[0, i - 1]
        else:
            tot = tot + lo_x[4]
        before = flows[0]
        total[i] = tot
        over = -DAMPING / tot
        for c in range(3):
            send(c, i, v[c, i, top, :], v[c, i, low, :])
            send(4 + c, i, coeff[c, i, top, :], coeff[c, i, low, :])
            own[c, row, :] = v[c, i, low, :]
            own[3 + c, row, :] = v[c, i, top, :]
        own[6, row, :] = p[i, low, :]
        own[7, row, :] = coeff[1, i, top, :]
        send(3, i, flows[1][top], p[i, low, :])
        send(7, i, right[top], right[low])
        send(8, i, over[top], right[near])
        send(9, i, zero, tot[low])
        send(10, i, zero, over[near])
    send(11, 0, before[top], before[low])
    send(11, 1, zero, before[near])
    for i in range(2, nx):
        send(11, i, zero, zero)


def extend(dst, index, own, r16, r17, low):
    n = own.shape[0]
    dst[index, 0:n, :] = own
    dst[index, n : n + 1, :] = r16
    dst[index, n + 1 : n + 2, :] = r17
    dst[index, EXT - 1 : EXT, :] = low


def whole_flux(c, i, flux0, coeff, prev, lo_x, hi_x, lo_y, hi_y, rows):
    nx, ny = flux0.shape[1], flux0.shape[2]
    first, last = rows == 0, rows == ny - 1
    row = slice(i, i + 1)
    k = coeff[c, i]
    near = jnp.where(first, lo_y[c, row, :], 0.0) + jnp.where(last, hi_y[c, row, :], 0.0)
    if i == 0:
        near = near + lo_x[c]
    if i == nx - 1:
        near = near + hi_x[c]
    value = flux0[c, i] + share(k) * near
    whole, _, lines, _ = ring_plan(nx, ny)
    if (c, i) not in whole:
        inside = (rows > 1) & (rows < ny - (2 if c == 1 else 1))
        value = value + k * jnp.where(inside, prev[c, i - 2], 0.0)
    if c == 0 and i == nx - 1:
        value = value - k * hi_x[3]
    if c == 1:
        value = value - k * jnp.where(last, hi_y[3, row, :], 0.0)
    return value


def whole_layer(i, flows, before, s, total, out_rows, lo_y, right_x, scale_x, index, first):
    ny = s.shape[1]
    row = slice(i, i + 1)
    right = flows[0] + flows[1] - jnp.where(first, out_rows[0, row, :], below_y(flows[1]))
    right = right + flows[2] - below_z(flows[2]) - s[i]
    if before is not None:
        right = right - before
    scale = -DAMPING / (total[i] + jnp.where(first, lo_y[5, row, :], 0.0))
    extend(
        right_x, index, right,
        out_rows[2, row, :] - flows[1][ny - 1 : ny], out_rows[3, row, :], out_rows[1, row, :],
    )
    extend(scale_x, index, scale, out_rows[4, row, :], out_rows[6, row, :], out_rows[5, row, :])


def strip_kernel(
    parity, flux0, coeff, s, total, lo_x, hi_x, got_odd, got_even, own,
    lo_y, hi_y, out_rows, send_odd, send_even, right_x, scale_x, side,
):
    nx, ny = s.shape[0], s.shape[1]
    even_x, even_y = parity[0] == 0, parity[1] == 0
    rows = row_id(s.shape[1:])
    first = rows == 0
    for layer in range(12):
        lo_y[layer], hi_y[layer] = pick(even_y, got_odd, got_even, layer)

    def along_x(x):
        return x - jnp.where(first_x, 0.0, pltpu.roll(x, 1, 0))

    first_x = row_id((nx, s.shape[2])) == 0
    edge = share(lo_y[4]) * own[0]
    push_y = share(lo_y[5]) * own[1] - lo_y[5] * own[6]
    push_z = share(lo_y[6]) * own[2]
    out_rows[0] = lo_y[3] + push_y
    out_rows[1] = lo_y[7] + along_x(edge) + push_y + push_z - below_z(push_z)
    out_rows[5] = lo_y[8]
    side_low = lo_y[11, 0:1, :] + edge[nx - 1 :]
    edge = share(hi_y[4]) * own[3]
    push_y = share(hi_y[5]) * own[4]
    push_z = share(hi_y[6]) * own[5]
    out_rows[2] = hi_y[7] + along_x(edge) + push_y + push_z - below_z(push_z)
    out_rows[3] = hi_y[8] - push_y
    out_rows[4] = -DAMPING / (hi_y[9] + own[7])
    out_rows[6] = hi_y[10]
    side_16, side_17 = hi_y[11, 0:1, :] + edge[nx - 1 :], hi_y[11, 1:2, :]

    right_x[...] = jnp.zeros_like(right_x)
    scale_x[...] = jnp.zeros_like(scale_x)
    side[...] = jnp.zeros_like(side)
    args = (flux0, coeff, None, lo_x, hi_x, lo_y, hi_y, rows)
    before = None
    for n, i in enumerate((0, 1, nx - 1)):
        if i == nx - 1:
            before = whole_flux(0, i - 1, *args)
        flows = [whole_flux(c, i, *args) for c in range(3)]
        whole_layer(i, flows, before, s, total, out_rows, lo_y, right_x, scale_x, n, first)
        before = flows[0]
    extend(side, 0, before, side_16, side_17, side_low)
    side[0, ny + 2 : ny + 3, :] = hi_y[4, nx - 1 : nx, :]
    scale_x[0, ny + 2 : ny + 3, :] = lo_y[5, 0:1, :]
    out_rows[7] = jnp.zeros(out_rows.shape[1:], jnp.float32)
    out_rows[7, 0:1, :] = side_low
    out_rows[7, 1:2, :] = side_16
    out_rows[7, 2:3, :] = side_17

    def send(layer, up, down):
        send_even[layer] = jnp.where(even_x, up, down)
        send_odd[layer] = jnp.where(even_x, down, up)

    send(0, right_x[2] * scale_x[2], right_x[1] * scale_x[1])
    send(1, side[0], right_x[0])
    send(2, jnp.zeros(side.shape[1:], jnp.float32), scale_x[0])


def own_kernel(
    flux0, coeff, prev, s, total, lo_x, hi_x, lo_y, hi_y, out_rows,
    flux, first_c, scale_x, side, kx, ky, kz,
):
    nx, ny = s.shape[0], s.shape[1]
    rows = row_id(s.shape[1:])
    first = rows == 0
    args = (flux0, coeff, prev, lo_x, hi_x, lo_y, hi_y, rows)
    zero = jnp.zeros((1, s.shape[2]), jnp.float32)
    for ref in (first_c, scale_x, side, kx, ky, kz):
        ref[...] = jnp.zeros_like(ref)
    before = None
    for i in range(nx):
        row = slice(i, i + 1)
        flows = [whole_flux(c, i, *args) for c in range(3)]
        for c in range(3):
            flux[c, i] = flows[c]
        whole_layer(i, flows, before, s, total, out_rows, lo_y, first_c, scale_x, i, first)
        first_c[i] = first_c[i] * scale_x[i]
        before = flows[0]
        extend(kx, i, coeff[0, i], hi_y[4, row, :], zero, zero)
        extend(ky, i, coeff[1, i], hi_y[5, row, :], zero, lo_y[5, row, :])
        extend(kz, i, coeff[2, i], hi_y[6, row, :], zero, zero)
    extend(side, 0, before, out_rows[7, 1:2, :], out_rows[7, 2:3, :], out_rows[7, 0:1, :])


def last_kernel(
    parity, flux, own_c, own_scale, side, own_kx, own_ky, own_kz, p, lo_x, hi_x, got_odd, got_even,
    new_v, new_p, edge,
):
    nx, ny = p.shape[0], p.shape[1]
    even_x = parity[0] == 0
    lo0, hi0 = pick(even_x, got_odd, got_even, 0)
    lo1, hi1 = pick(even_x, got_odd, got_even, 1)
    _, hi2 = pick(even_x, got_odd, got_even, 2)
    edge[...] = jnp.zeros_like(edge)
    edge[0, 0:ny, :] = lo_x[4]
    edge[0, ny : ny + 1, :] = lo1[ny + 2 : ny + 3, :]
    edge[1, 0:ny, :] = hi_x[4]
    edge[2, 0:ny, :] = hi_x[5]
    edge[2, EXT - 1 : EXT, :] = hi2[ny + 2 : ny + 3, :]
    edge[3, 0:ny, :] = hi_x[6]

    def first_c(i):
        if i == -1:
            return lo0
        if i == 0:
            return own_c[0] - lo1 * own_scale[0]
        if i == nx:
            return (hi1 - side[0]) * hi2
        if i == nx + 1:
            return hi0
        return own_c[i]

    def sweep(i, low, mid, high):
        if i < nx:
            kx, ky, kz, scale = own_kx[i], own_ky[i], own_kz[i], own_scale[i]
        else:
            kx, ky, kz, scale = edge[1], edge[2], edge[3], hi2
        below_kx = own_kx[i - 1] if i > 0 else edge[0]
        gx = kx * (high - mid) - below_kx * (mid - low)
        gy = ky * (above_y(mid) - mid)
        gz = kz * (above_z(mid) - mid)
        applied = gx + gy - below_y(gy) + gz - below_z(gz)
        return 2.0 * mid - scale * applied

    low, mid, high = first_c(-1), first_c(0), first_c(1)
    now = sweep(0, low, mid, high)
    for i in range(nx):
        low, mid, high = mid, high, first_c(i + 2)
        after = sweep(i + 1, low, mid, high)
        new_p[i] = p[i] + now[:ny]
        new_v[0, i] = flux[0, i] - own_kx[i, :ny] * (after - now)[:ny]
        new_v[1, i] = flux[1, i] - own_ky[i, :ny] * (above_y(now) - now)[:ny]
        new_v[2, i] = flux[2, i] - own_kz[i, :ny] * (above_z(now) - now)[:ny]
        now = after


VM = pl.BlockSpec(memory_space=pltpu.VMEM)
SM = pl.BlockSpec(memory_space=pltpu.SMEM)


def call(kernel, args, outs, scratch=(), scalars=True, flops=1000):
    shapes = [jax.ShapeDtypeStruct(s, jnp.float32) for s in outs]
    size = sum(4 * a.size for a in args) + sum(4 * s.size for s in shapes)
    specs = [SM] + [VM] * (len(args) - 1) if scalars else [VM] * len(args)
    return pl.pallas_call(
        kernel,
        out_shape=shapes,
        in_specs=specs,
        out_specs=[VM] * len(shapes),
        scratch_shapes=[pltpu.VMEM(s, jnp.float32) for s in scratch],
        compiler_params=pltpu.CompilerParams(vmem_limit_bytes=40 * 2**20),
        cost_estimate=pl.CostEstimate(flops=flops, bytes_accessed=size, transcendentals=0),
    )(*args)


def body(velocity, pressure, forcing, source, viscosity):
    v, p, f, s = velocity[:, 0], pressure[0], forcing[:, 0], source[0]
    nx, ny, nz = p.shape
    steps = lax.axis_size("ta")
    ahead = [(i, i + 1) for i in range(steps - 1)]
    parity = jnp.stack([lax.axis_index("gx") % 2, lax.axis_index("gy") % 2]).astype(jnp.int32)
    (ring,) = call(ring_kernel, (v,), ((ring_plan(nx, ny)[3], ny, nz),), scalars=False, flops=20_000_000_000)
    face_odd, face_even = call(face_kernel, (parity, v, p, viscosity), ((7, ny, nz), (7, ny, nz)), flops=20_000_000_000)
    odd_x, even_x = swap_odd(face_odd, "gx"), swap_even(face_even, "gx")
    ring = lax.ppermute(ring, "ta", ahead)
    flux0, coeff = call(local_kernel, (v, p, f, viscosity, ring), (v.shape,) * 2, scalars=False)
    lo_x, hi_x, total, send_odd, send_even, own, inner = call(
        edge_kernel,
        (parity, flux0, coeff, v, p, s, odd_x, even_x),
        ((7, ny, nz), (7, ny, nz), p.shape, (12, nx, nz), (12, nx, nz), (8, nx, nz), (3, nx - 3, ny, nz)),
    )
    prev = lax.ppermute(inner, "ta", ahead)
    odd_y, even_y = swap_odd(send_odd, "gy"), swap_even(send_even, "gy")
    lo_y, hi_y, out_rows, send_odd, send_even = call(
        strip_kernel,
        (parity, flux0, coeff, s, total, lo_x, hi_x, odd_y, even_y, own),
        ((12, nx, nz), (12, nx, nz), (8, nx, nz), (3, EXT, nz), (3, EXT, nz)),
        ((3, EXT, nz), (3, EXT, nz), (1, EXT, nz)),
        flops=20_000_000_000,
    )
    odd_x, even_x = swap_odd(send_odd, "gx"), swap_even(send_even, "gx")
    flux, first_c, scale, side, kx, ky, kz = call(
        own_kernel,
        (flux0, coeff, prev, s, total, lo_x, hi_x, lo_y, hi_y, out_rows),
        (v.shape, (nx, EXT, nz), (nx, EXT, nz), (1, EXT, nz)) + ((nx, EXT, nz),) * 3,
        scalars=False,
    )
    new_v, new_p = call(
        last_kernel,
        (parity, flux, first_c, scale, side, kx, ky, kz, p, lo_x, hi_x, odd_x, even_x),
        (v.shape, p.shape),
        ((4, EXT, nz),),
    )
    return new_v[:, None], new_p[None]


def solution(mesh):
    placed = (
        P(None, "ta", "gx", "gy", None),
        P("ta", "gx", "gy", None),
        P(None, "ta", "gx", "gy", None),
        P("ta", "gx", "gy", None),
        P(None, "gx", "gy", None),
    )
    return jax.shard_map(
        body,
        mesh=mesh,
        in_specs=placed,
        out_specs=(P(None, "ta", "gx", "gy", None), P("ta", "gx", "gy", None)),
        check_vma=False,
    )
```

```python
import jax
import jax.numpy as jnp
from jax import lax
from jax.experimental import pallas as pl
from jax.experimental.pallas import tpu as pltpu
from jax.sharding import PartitionSpec as P

RELAX = 1.5
DAMPING = 0.8
EXT = 24


def odd_pairs(n):
    return [p for i in range(1, n, 2) for p in ((i, (i + 1) % n), ((i + 1) % n, i))]


def even_pairs(n):
    return [p for i in range(0, n, 2) for p in ((i, i + 1), (i + 1, i))]


def swap_odd(x, axis):
    return lax.ppermute(x, axis, odd_pairs(lax.axis_size(axis)))


def swap_even(x, axis):
    return lax.ppermute(x, axis, even_pairs(lax.axis_size(axis)))


def above_z(x):
    return pltpu.roll(x, x.shape[1] - 1, 1)


def below_z(x):
    return pltpu.roll(x, 1, 1)


def above_y(x):
    return pltpu.roll(x, x.shape[0] - 1, 0)


def below_y(x):
    return pltpu.roll(x, 1, 0)


def row_id(shape):
    return lax.broadcasted_iota(jnp.int32, shape, 0)


def coeff_of(visc):
    return 1.0 / (RELAX * (1.0 + 6.0 * visc))


def ring_plan(nx, ny):
    layers = [(c, i) for c in range(3) for i in (0, 1, nx - 1)] + [(0, nx - 2)]
    whole = {key: tile for tile, key in enumerate(layers)}
    lines = [(0, 1, ny - 1), (0, 1, ny - 2, ny - 1), (0, 1, ny - 1)]
    single = {}
    for c in range(3):
        for i in range(nx):
            if (c, i) not in whole:
                for j in lines[c]:
                    tile, row = divmod(len(single), ny)
                    single[c, i, j] = (len(whole) + tile, row)
    return whole, single, lines, len(whole) + -(-len(single) // ny)


def bulk_plan(nx, ny):
    whole = ring_plan(nx, ny)[0]
    start, used = {}, 2
    for c in range(3):
        for i in range(nx):
            if (c, i) not in whole:
                start[c, i] = used
                used += inner_rows(c, ny)
    return start, -(-(used + 4) // 8) * 8


def inner_rows(c, ny):
    return ny - (4 if c == 1 else 3)


def share(c):
    return (1.0 / RELAX - c) * (1.0 / 6.0)


def pick(even, odd_got, even_got, index):
    a, b = odd_got[index], even_got[index]
    return jnp.where(even, a, b), jnp.where(even, b, a)


def ring_kernel(v, ring):
    nx, ny = v.shape[1], v.shape[2]
    whole, single, _, tiles = ring_plan(nx, ny)
    ring[tiles - 1] = jnp.zeros(ring.shape[1:], jnp.float32)
    for (c, i), tile in whole.items():
        ring[tile] = v[c, i]
    for (c, i, j), (tile, row) in single.items():
        ring[tile, row : row + 1, :] = v[c, i, j : j + 1, :]


def face_kernel(parity, v, p, visc, send_odd, send_even):
    nx = v.shape[1]
    even_x = parity[0] == 0

    def send(layer, up, down):
        send_even[layer] = jnp.where(even_x, up, down)
        send_odd[layer] = jnp.where(even_x, down, up)

    for c in range(3):
        send(c, v[c, nx - 1], v[c, 0])
        send(4 + c, coeff_of(visc[c, nx - 1]), coeff_of(visc[c, 0]))
    send(3, jnp.zeros(p.shape[1:], jnp.float32), p[0])


def local_kernel(v, p, f, visc, ring, flux, coeff):
    nx, ny = p.shape[0], p.shape[1]
    rows = row_id(p.shape[1:])
    first, last = rows == 0, rows == ny - 1
    whole, single, lines, _ = ring_plan(nx, ny)
    for i in range(nx):
        pressure = p[i]
        slope_x = (p[i + 1] if i + 1 < nx else jnp.zeros_like(pressure)) - pressure
        slope_y = jnp.where(last, 0.0, above_y(pressure)) - pressure
        slope_z = above_z(pressure) - pressure
        for c, slope in enumerate((slope_x, slope_y, slope_z)):
            nu = visc[c, i]
            k = coeff_of(nu)
            flow = v[c, i]
            near = above_z(flow) + below_z(flow)
            near = near + jnp.where(last, 0.0, above_y(flow)) + jnp.where(first, 0.0, below_y(flow))
            if i > 0:
                near = near + v[c, i - 1]
            if i + 1 < nx:
                near = near + v[c, i + 1]
            coeff[c, i] = k
            if (c, i) in whole:
                prev = ring[whole[c, i]]
            else:
                prev = jnp.zeros(p.shape[1:], jnp.float32)
                for j in lines[c]:
                    tile, row = single[c, i, j]
                    prev = jnp.where(rows == j, ring[tile, row : row + 1, :], prev)
            flux[c, i] = k * (f[c, i] + prev + nu * near - slope) + flow * (1.0 - 1.0 / RELAX)


def edge_kernel(parity, flux0, coeff, v, p, s, got_odd, got_even, lo_x, hi_x, total, send_odd, send_even, own):
    nx, ny = s.shape[0], s.shape[1]
    shape = s.shape[1:]
    rows = row_id(shape)
    first = rows == 0
    even_y = parity[1] == 0
    zero = jnp.zeros((1, shape[1]), jnp.float32)
    top, low, near = slice(ny - 1, ny), slice(0, 1), slice(1, 2)
    for layer in range(7):
        lo_x[layer], hi_x[layer] = pick(parity[0] == 0, got_odd, got_even, layer)

    def send(layer, i, up, down):
        row = layer * nx + i
        send_even[row : row + 1, :] = jnp.where(even_y, up, down)
        send_odd[row : row + 1, :] = jnp.where(even_y, down, up)

    before = None
    for i in range(nx):
        row = slice(i, i + 1)
        flows = []
        for c in range(3):
            k = coeff[c, i]
            value = flux0[c, i]
            if i == 0:
                value = value + share(k) * lo_x[c]
            if i == nx - 1:
                value = value + share(k) * hi_x[c]
                if c == 0:
                    value = value - k * hi_x[3]
            flows.append(value)
        right = flows[0] + flows[1] - jnp.where(first, 0.0, below_y(flows[1])) + flows[2] - below_z(flows[2])
        right = right - s[i]
        kx, ky, kz = coeff[0, i], coeff[1, i], coeff[2, i]
        tot = kx + ky + jnp.where(first, 0.0, below_y(ky)) + kz + below_z(kz)
        if i > 0:
            right = right - before
            tot = tot + coeff[0, i - 1]
        else:
            tot = tot + lo_x[4]
        before = flows[0]
        total[i] = tot
        over = -DAMPING / tot
        for c in range(3):
            send(c, i, v[c, i, top, :], v[c, i, low, :])
            send(4 + c, i, coeff[c, i, top, :], coeff[c, i, low, :])
            own[c, row, :] = v[c, i, low, :]
            own[3 + c, row, :] = v[c, i, top, :]
        own[6, row, :] = p[i, low, :]
        own[7, row, :] = coeff[1, i, top, :]
        send(3, i, flows[1][top], p[i, low, :])
        send(7, i, right[top], right[low])
        send(8, i, over[top], right[near])
        send(9, i, zero, over[near])
    send(10, 0, before[top], before[low])
    send(10, 1, zero, before[near])
    send(10, 2, zero, lo_x[4, low, :])
    for i in range(3, 8):
        send(10, i, zero, zero)


def extend(dst, index, own, r16, r17, low):
    n = own.shape[0]
    dst[index, 0:n, :] = own
    dst[index, n : n + 1, :] = r16
    dst[index, n + 1 : n + 2, :] = r17
    dst[index, EXT - 1 : EXT, :] = low


def bulk_kernel(v, _, bulk):
    ny = v.shape[2]
    start, size = bulk_plan(v.shape[1], ny)
    bulk[0:8, :] = jnp.zeros((8, bulk.shape[1]), jnp.float32)
    bulk[size - 8 :, :] = jnp.zeros((8, bulk.shape[1]), jnp.float32)
    for (c, i), row in start.items():
        count = inner_rows(c, ny)
        bulk[row : row + count, :] = v[c, i, 2 : 2 + count, :]


def whole_flux(c, i, flux0, coeff, prev, lo_x, hi_x, lo_y, hi_y, rows):
    nx, ny = flux0.shape[1], flux0.shape[2]
    first, last = rows == 0, rows == ny - 1
    row = slice(i, i + 1)
    k = coeff[c, i]
    near = jnp.where(first, lo_y[c, row, :], 0.0) + jnp.where(last, hi_y[c, row, :], 0.0)
    if i == 0:
        near = near + lo_x[c]
    if i == nx - 1:
        near = near + hi_x[c]
    value = flux0[c, i] + share(k) * near
    if (c, i) not in ring_plan(nx, ny)[0]:
        inside = (rows > 1) & (rows < ny - (2 if c == 1 else 1))
        begin = bulk_plan(nx, ny)[0][c, i] - 2
        value = value + k * jnp.where(inside, prev[begin : begin + ny, :], 0.0)
    if c == 0 and i == nx - 1:
        value = value - k * hi_x[3]
    if c == 1:
        value = value - k * jnp.where(last, hi_y[3, row, :], 0.0)
    return value


def whole_layer(i, flows, before, s, total, out_rows, lo_y, right_x, scale_x, index, first):
    ny = s.shape[1]
    row = slice(i, i + 1)
    right = flows[0] + flows[1] - jnp.where(first, out_rows[0, row, :], below_y(flows[1]))
    right = right + flows[2] - below_z(flows[2]) - s[i]
    if before is not None:
        right = right - before
    scale = -DAMPING / (total[i] + jnp.where(first, lo_y[5, row, :], 0.0))
    extend(
        right_x, index, right,
        out_rows[2, row, :] - flows[1][ny - 1 : ny], out_rows[3, row, :], out_rows[1, row, :],
    )
    extend(scale_x, index, scale, out_rows[4, row, :], out_rows[6, row, :], out_rows[5, row, :])


def strip_kernel(
    parity, flux0, coeff, s, total, lo_x, hi_x, got_odd, got_even, own,
    lo_y, hi_y, out_rows, send_odd, send_even, right_x, scale_x, side,
):
    nx, ny = s.shape[0], s.shape[1]
    even_x, even_y = parity[0] == 0, parity[1] == 0
    rows = row_id(s.shape[1:])
    first = rows == 0
    for layer in range(10):
        lo_y[layer], hi_y[layer] = pick(even_y, got_odd, got_even, slice(layer * nx, layer * nx + nx))
    lo_few, hi_few = pick(even_y, got_odd, got_even, slice(10 * nx, 10 * nx + 8))

    def along_x(x):
        return x - jnp.where(first_x, 0.0, pltpu.roll(x, 1, 0))

    first_x = row_id((nx, s.shape[2])) == 0
    edge = share(lo_y[4]) * own[0]
    push_y = share(lo_y[5]) * own[1] - lo_y[5] * own[6]
    push_z = share(lo_y[6]) * own[2]
    out_rows[0] = lo_y[3] + push_y
    out_rows[1] = lo_y[7] + along_x(edge) + push_y + push_z - below_z(push_z)
    out_rows[5] = lo_y[8]
    side_low = lo_few[0:1] + edge[nx - 1 :]
    edge = share(hi_y[4]) * own[3]
    push_y = share(hi_y[5]) * own[4]
    push_z = share(hi_y[6]) * own[5]
    out_rows[2] = hi_y[7] + along_x(edge) + push_y + push_z - below_z(push_z)
    out_rows[3] = hi_y[8] - push_y
    before = jnp.where(first_x, hi_few[2:3], pltpu.roll(hi_y[4], 1, 0))
    out_rows[4] = -DAMPING / (hi_y[4] + before + hi_y[5] + own[7] + hi_y[6] + below_z(hi_y[6]))
    out_rows[6] = hi_y[9]
    side_16, side_17 = hi_few[0:1] + edge[nx - 1 :], hi_few[1:2]

    right_x[...] = jnp.zeros_like(right_x)
    scale_x[...] = jnp.zeros_like(scale_x)
    side[...] = jnp.zeros_like(side)
    args = (flux0, coeff, None, lo_x, hi_x, lo_y, hi_y, rows)
    before = None
    for n, i in enumerate((0, 1, nx - 1)):
        if i == nx - 1:
            before = whole_flux(0, i - 1, *args)
        flows = [whole_flux(c, i, *args) for c in range(3)]
        whole_layer(i, flows, before, s, total, out_rows, lo_y, right_x, scale_x, n, first)
        before = flows[0]
    extend(side, 0, before, side_16, side_17, side_low)
    side[0, ny + 2 : ny + 3, :] = hi_y[4, nx - 1 : nx, :]
    scale_x[0, ny + 2 : ny + 3, :] = lo_y[5, 0:1, :]
    out_rows[7] = jnp.zeros(out_rows.shape[1:], jnp.float32)
    out_rows[7, 0:1, :] = side_low
    out_rows[7, 1:2, :] = side_16
    out_rows[7, 2:3, :] = side_17

    def send(layer, up, down):
        send_even[layer] = jnp.where(even_x, up, down)
        send_odd[layer] = jnp.where(even_x, down, up)

    send(0, right_x[2] * scale_x[2], right_x[1] * scale_x[1])
    send(1, side[0], right_x[0])
    send(2, jnp.zeros(side.shape[1:], jnp.float32), scale_x[0])


def sweep(low, mid, high, below_kx, kx, ky, kz, scale):
    gx = kx * (high - mid) - below_kx * (mid - low)
    gy = ky * (above_y(mid) - mid)
    gz = kz * (above_z(mid) - mid)
    applied = gx + gy - below_y(gy) + gz - below_z(gz)
    return 2.0 * mid - scale * applied


def own_kernel(
    flux0, coeff, prev, s, p, total, lo_x, hi_x, lo_y, hi_y, out_rows,
    flux, first_c, scale_x, side, kx, ky, kz, ends, wide_v, wide_p,
):
    nx, ny = s.shape[0], s.shape[1]
    rows = row_id(s.shape[1:])
    first = rows == 0
    args = (flux0, coeff, prev, lo_x, hi_x, lo_y, hi_y, rows)
    zero = jnp.zeros((1, s.shape[2]), jnp.float32)
    for ref in (first_c, scale_x, side, kx, ky, kz):
        ref[...] = jnp.zeros_like(ref)
    before = None
    for i in range(nx):
        row = slice(i, i + 1)
        flows = [whole_flux(c, i, *args) for c in range(3)]
        for c in range(3):
            flux[c, i] = flows[c]
        whole_layer(i, flows, before, s, total, out_rows, lo_y, first_c, scale_x, i, first)
        first_c[i] = first_c[i] * scale_x[i]
        before = flows[0]
        extend(kx, i, coeff[0, i], hi_y[4, row, :], zero, zero)
        extend(ky, i, coeff[1, i], hi_y[5, row, :], zero, lo_y[5, row, :])
        extend(kz, i, coeff[2, i], hi_y[6, row, :], zero, zero)
    extend(side, 0, before, out_rows[7, 1:2, :], out_rows[7, 2:3, :], out_rows[7, 0:1, :])
    now = None
    for i in range(2, nx - 1):
        after = sweep(first_c[i - 1], first_c[i], first_c[i + 1], kx[i - 1], kx[i], ky[i], kz[i], scale_x[i])
        wide_p[i - 2] = p[i] + after[:ny]
        wide_v[1, i - 2] = flux[1, i] - coeff[1, i] * (above_y(after) - after)[:ny]
        wide_v[2, i - 2] = flux[2, i] - coeff[2, i] * (above_z(after) - after)[:ny]
        if now is None:
            ends[0] = after
        else:
            wide_v[0, i - 3] = flux[0, i - 1] - coeff[0, i - 1] * (after - now)[:ny]
        now = after
    ends[1] = now


def last_kernel(
    parity, flux, own_c, own_scale, side, own_kx, own_ky, own_kz, ends, p, lo_x, hi_x, got_odd, got_even, wide_v, wide_p,
    new_v, new_p, edge, low_v, low_p, top_v, top_p, top_x, sems,
):
    nx, ny = p.shape[0], p.shape[1]
    ready = [
        pltpu.make_async_copy(wide_v.at[0, pl.ds(0, nx - 4)], new_v.at[0, pl.ds(2, nx - 4)], sems.at[5]),
        pltpu.make_async_copy(wide_v.at[1], new_v.at[1, pl.ds(2, nx - 3)], sems.at[6]),
        pltpu.make_async_copy(wide_v.at[2], new_v.at[2, pl.ds(2, nx - 3)], sems.at[7]),
        pltpu.make_async_copy(wide_p, new_p.at[pl.ds(2, nx - 3)], sems.at[8]),
    ]
    for copy in ready:
        copy.start()
    even_x = parity[0] == 0
    lo0, hi0 = pick(even_x, got_odd, got_even, 0)
    lo1, hi1 = pick(even_x, got_odd, got_even, 1)
    _, hi2 = pick(even_x, got_odd, got_even, 2)
    edge[...] = jnp.zeros_like(edge)
    edge[0, 0:ny, :] = lo_x[4]
    edge[0, ny : ny + 1, :] = lo1[ny + 2 : ny + 3, :]
    edge[1, 0:ny, :] = hi_x[4]
    edge[2, 0:ny, :] = hi_x[5]
    edge[2, EXT - 1 : EXT, :] = hi2[ny + 2 : ny + 3, :]
    edge[3, 0:ny, :] = hi_x[6]
    zeroth = own_c[0] - lo1 * own_scale[0]
    beyond = (hi1 - side[0]) * hi2
    at = lambda i: (own_kx[i], own_ky[i], own_kz[i], own_scale[i])
    second = {
        0: sweep(lo0, zeroth, own_c[1], edge[0], *at(0)),
        1: sweep(zeroth, own_c[1], own_c[2], own_kx[0], *at(1)),
        2: ends[0],
        nx - 2: ends[1],
        nx - 1: sweep(own_c[nx - 2], own_c[nx - 1], beyond, own_kx[nx - 2], *at(nx - 1)),
        nx: sweep(own_c[nx - 1], beyond, hi0, own_kx[nx - 1], edge[1], edge[2], edge[3], hi2),
    }

    def step_x(i):
        return flux[0, i] - own_kx[i, :ny] * (second[i + 1] - second[i])[:ny]

    def step_y(i):
        return flux[1, i] - own_ky[i, :ny] * (above_y(second[i]) - second[i])[:ny]

    def step_z(i):
        return flux[2, i] - own_kz[i, :ny] * (above_z(second[i]) - second[i])[:ny]

    for n, i in enumerate((0, 1)):
        low_v[0, n], low_v[1, n], low_v[2, n] = step_x(i), step_y(i), step_z(i)
        low_p[n] = p[i] + second[i][:ny]
    top_v[0, 0], top_v[1, 0], top_v[2, 0] = step_x(nx - 1), step_y(nx - 1), step_z(nx - 1)
    top_p[0] = p[nx - 1] + second[nx - 1][:ny]
    top_x[0] = step_x(nx - 2)
    copies = [
        pltpu.make_async_copy(low_v, new_v.at[:, pl.ds(0, 2)], sems.at[0]),
        pltpu.make_async_copy(top_v, new_v.at[:, pl.ds(nx - 1, 1)], sems.at[1]),
        pltpu.make_async_copy(top_x, new_v.at[0, pl.ds(nx - 2, 1)], sems.at[2]),
        pltpu.make_async_copy(low_p, new_p.at[pl.ds(0, 2)], sems.at[3]),
        pltpu.make_async_copy(top_p, new_p.at[pl.ds(nx - 1, 1)], sems.at[4]),
    ]
    for copy in copies:
        copy.start()
    for copy in ready + copies:
        copy.wait()


VM = pl.BlockSpec(memory_space=pltpu.VMEM)
SM = pl.BlockSpec(memory_space=pltpu.SMEM)


ANY = pl.BlockSpec(memory_space=pl.ANY)


def call(kernel, args, outs, scratch=(), scalars=True, flops=1000, far=0):
    shapes = [jax.ShapeDtypeStruct(s, jnp.float32) for s in outs]
    size = sum(4 * a.size for a in args) + sum(4 * s.size for s in shapes)
    return pl.pallas_call(
        kernel,
        out_shape=shapes,
        in_specs=[SM] * scalars + [VM] * (len(args) - scalars),
        out_specs=[VM] * (len(shapes) - far) + [ANY] * far,
        scratch_shapes=[pltpu.VMEM(s, jnp.float32) for s in scratch] + [pltpu.SemaphoreType.DMA((9,))] * (far > 0),
        compiler_params=pltpu.CompilerParams(vmem_limit_bytes=40 * 2**20),
        cost_estimate=pl.CostEstimate(flops=flops, bytes_accessed=size, transcendentals=0),
    )(*args)


def body(velocity, pressure, forcing, source, viscosity):
    v, p, f, s = velocity[:, 0], pressure[0], forcing[:, 0], source[0]
    nx, ny, nz = p.shape
    steps = lax.axis_size("ta")
    ahead = [(i, i + 1) for i in range(steps - 1)]
    parity = jnp.stack([lax.axis_index("gx") % 2, lax.axis_index("gy") % 2]).astype(jnp.int32)
    (ring,) = call(ring_kernel, (v,), ((ring_plan(nx, ny)[3], ny, nz),), scalars=False, flops=20_000_000_000)
    face_odd, face_even = call(face_kernel, (parity, v, p, viscosity), ((7, ny, nz), (7, ny, nz)), flops=20_000_000_000)
    odd_x, even_x = swap_odd(face_odd, "gx"), swap_even(face_even, "gx")
    ring = lax.ppermute(ring, "ta", ahead)
    flux0, coeff = call(local_kernel, (v, p, f, viscosity, ring), (v.shape,) * 2, scalars=False)
    lo_x, hi_x, total, send_odd, send_even, own = call(
        edge_kernel,
        (parity, flux0, coeff, v, p, s, odd_x, even_x),
        ((7, ny, nz), (7, ny, nz), p.shape, (10 * nx + 8, nz), (10 * nx + 8, nz), (8, nx, nz)),
    )
    (bulk,) = call(bulk_kernel, (v, total), ((bulk_plan(nx, ny)[1], nz),), scalars=False)
    prev = lax.ppermute(bulk, "ta", ahead)
    odd_y, even_y = swap_odd(send_odd, "gy"), swap_even(send_even, "gy")
    lo_y, hi_y, out_rows, send_odd, send_even = call(
        strip_kernel,
        (parity, flux0, coeff, s, total, lo_x, hi_x, odd_y, even_y, own),
        ((10, nx, nz), (10, nx, nz), (8, nx, nz), (3, EXT, nz), (3, EXT, nz)),
        ((3, EXT, nz), (3, EXT, nz), (1, EXT, nz)),
        flops=20_000_000_000,
    )
    odd_x, even_x = swap_odd(send_odd, "gx"), swap_even(send_even, "gx")
    flux, first_c, scale, side, kx, ky, kz, ends, wide_v, wide_p = call(
        own_kernel,
        (flux0, coeff, prev, s, p, total, lo_x, hi_x, lo_y, hi_y, out_rows),
        (v.shape, (nx, EXT, nz), (nx, EXT, nz), (1, EXT, nz))
        + ((nx, EXT, nz),) * 3
        + ((2, EXT, nz), (3, nx - 3, ny, nz), (nx - 3, ny, nz)),
        scalars=False,
    )
    new_v, new_p = call(
        last_kernel,
        (parity, flux, first_c, scale, side, kx, ky, kz, ends, p, lo_x, hi_x, odd_x, even_x, wide_v, wide_p),
        (v.shape, p.shape),
        ((4, EXT, nz), (3, 2, ny, nz), (2, ny, nz), (3, 1, ny, nz), (1, ny, nz), (1, ny, nz)),
        far=2,
    )
    return new_v[:, None], new_p[None]


def solution(mesh):
    placed = (
        P(None, "ta", "gx", "gy", None),
        P("ta", "gx", "gy", None),
        P(None, "ta", "gx", "gy", None),
        P("ta", "gx", "gy", None),
        P(None, "gx", "gy", None),
    )
    return jax.shard_map(
        body,
        mesh=mesh,
        in_specs=placed,
        out_specs=(P(None, "ta", "gx", "gy", None), P("ta", "gx", "gy", None)),
        check_vma=False,
    )
```

```python
import jax
import jax.numpy as jnp
from jax import lax
from jax.experimental import pallas as pl
from jax.experimental.pallas import tpu as pltpu
from jax.sharding import PartitionSpec as P

RELAX = 1.5
DAMPING = 0.8
MORE = 3
EXT = 24


def odd_pairs(n):
    return [p for i in range(1, n, 2) for p in ((i, (i + 1) % n), ((i + 1) % n, i))]


def even_pairs(n):
    return [p for i in range(0, n, 2) for p in ((i, i + 1), (i + 1, i))]


def swap_odd(x, axis):
    return lax.ppermute(x, axis, odd_pairs(lax.axis_size(axis)))


def swap_even(x, axis):
    return lax.ppermute(x, axis, even_pairs(lax.axis_size(axis)))


def is_even(axis):
    return lax.rem(lax.axis_index(axis), 2) == 0


def above_z(x):
    return pltpu.roll(x, x.shape[1] - 1, 1)


def below_z(x):
    return pltpu.roll(x, 1, 1)


def above_y(x):
    return pltpu.roll(x, x.shape[0] - 1, 0)


def below_y(x):
    return pltpu.roll(x, 1, 0)


def row_id(shape):
    return lax.broadcasted_iota(jnp.int32, shape, 0)


def coeff_of(visc):
    return 1.0 / (RELAX * (1.0 + 6.0 * visc))


def ring_plan(nx, ny):
    layers = [(c, i) for c in range(3) for i in (*range(2 + MORE), nx - 1)] + [(0, nx - 2)]
    whole = {key: tile for tile, key in enumerate(layers)}
    lines = [(0, 1, ny - 1), (0, 1, ny - 2, ny - 1), (0, 1, ny - 1)]
    single = {}
    for c in range(3):
        for i in range(nx):
            if (c, i) not in whole:
                for j in lines[c]:
                    tile, row = divmod(len(single), ny)
                    single[c, i, j] = (len(whole) + tile, row)
    return whole, single, lines, len(whole) + -(-len(single) // ny)


def bulk_plan(nx, ny):
    whole = ring_plan(nx, ny)[0]
    start, used = {}, 2
    for c in range(3):
        for i in range(nx):
            if (c, i) not in whole:
                start[c, i] = used
                used += inner_rows(c, ny)
    return start, -(-(used + 4) // 8) * 8


def inner_rows(c, ny):
    return ny - (4 if c == 1 else 3)


def share(c):
    return (1.0 / RELAX - c) * (1.0 / 6.0)


def pick(even, odd_got, even_got, index):
    a, b = odd_got[index], even_got[index]
    return jnp.where(even, a, b), jnp.where(even, b, a)


def ring_kernel(v, ring):
    nx, ny = v.shape[1], v.shape[2]
    whole, single, _, tiles = ring_plan(nx, ny)
    ring[tiles - 1] = jnp.zeros(ring.shape[1:], jnp.float32)
    for (c, i), tile in whole.items():
        ring[tile] = v[c, i]
    for (c, i, j), (tile, row) in single.items():
        ring[tile, row : row + 1, :] = v[c, i, j : j + 1, :]


def face_kernel(v, p, visc, send_odd, send_even):
    nx = v.shape[1]
    even_x = is_even("gx")

    def send(layer, up, down):
        send_even[layer] = jnp.where(even_x, up, down)
        send_odd[layer] = jnp.where(even_x, down, up)

    for c in range(3):
        send(c, v[c, nx - 1], v[c, 0])
        send(4 + c, coeff_of(visc[c, nx - 1]), coeff_of(visc[c, 0]))
    send(3, jnp.zeros(p.shape[1:], jnp.float32), p[0])


def local_kernel(v, p, f, visc, ring, flux, coeff):
    nx, ny = p.shape[0], p.shape[1]
    rows = row_id(p.shape[1:])
    first, last = rows == 0, rows == ny - 1
    whole, single, lines, _ = ring_plan(nx, ny)
    for i in range(nx):
        pressure = p[i]
        slope_x = (p[i + 1] if i + 1 < nx else jnp.zeros_like(pressure)) - pressure
        slope_y = jnp.where(last, 0.0, above_y(pressure)) - pressure
        slope_z = above_z(pressure) - pressure
        for c, slope in enumerate((slope_x, slope_y, slope_z)):
            nu = visc[c, i]
            k = coeff_of(nu)
            flow = v[c, i]
            near = above_z(flow) + below_z(flow)
            near = near + jnp.where(last, 0.0, above_y(flow)) + jnp.where(first, 0.0, below_y(flow))
            if i > 0:
                near = near + v[c, i - 1]
            if i + 1 < nx:
                near = near + v[c, i + 1]
            coeff[c, i] = k
            if (c, i) in whole:
                prev = ring[whole[c, i]]
            else:
                prev = jnp.zeros(p.shape[1:], jnp.float32)
                for j in lines[c]:
                    tile, row = single[c, i, j]
                    prev = jnp.where(rows == j, ring[tile, row : row + 1, :], prev)
            flux[c, i] = k * (f[c, i] + prev + nu * near - slope) + flow * (1.0 - 1.0 / RELAX)


def edge_kernel(flux0, coeff, v, p, s, got_odd, got_even, lo_x, hi_x, total, send_odd, send_even, own):
    nx, ny = s.shape[0], s.shape[1]
    shape = s.shape[1:]
    rows = row_id(shape)
    first = rows == 0
    even_y = is_even("gy")
    zero = jnp.zeros((1, shape[1]), jnp.float32)
    top, low, near = slice(ny - 1, ny), slice(0, 1), slice(1, 2)
    for layer in range(7):
        lo_x[layer], hi_x[layer] = pick(is_even("gx"), got_odd, got_even, layer)

    def send(layer, i, up, down):
        row = layer * nx + i
        send_even[row : row + 1, :] = jnp.where(even_y, up, down)
        send_odd[row : row + 1, :] = jnp.where(even_y, down, up)

    before = None
    for i in range(nx):
        row = slice(i, i + 1)
        flows = []
        for c in range(3):
            k = coeff[c, i]
            value = flux0[c, i]
            if i == 0:
                value = value + share(k) * lo_x[c]
            if i == nx - 1:
                value = value + share(k) * hi_x[c]
                if c == 0:
                    value = value - k * hi_x[3]
            flows.append(value)
        right = flows[0] + flows[1] - jnp.where(first, 0.0, below_y(flows[1])) + flows[2] - below_z(flows[2])
        right = right - s[i]
        kx, ky, kz = coeff[0, i], coeff[1, i], coeff[2, i]
        tot = kx + ky + jnp.where(first, 0.0, below_y(ky)) + kz + below_z(kz)
        if i > 0:
            right = right - before
            tot = tot + coeff[0, i - 1]
        else:
            tot = tot + lo_x[4]
        before = flows[0]
        total[i] = tot
        over = -DAMPING / tot
        for c in range(3):
            send(c, i, v[c, i, top, :], v[c, i, low, :])
            send(4 + c, i, coeff[c, i, top, :], coeff[c, i, low, :])
            own[c, row, :] = v[c, i, low, :]
            own[3 + c, row, :] = v[c, i, top, :]
        own[6, row, :] = p[i, low, :]
        own[7, row, :] = coeff[1, i, top, :]
        send(3, i, flows[1][top], p[i, low, :])
        send(7, i, right[top], right[low])
        send(8, i, over[top], right[near])
        send(9, i, zero, over[near])
    send(10, 0, before[top], before[low])
    send(10, 1, zero, before[near])
    send(10, 2, zero, lo_x[4, low, :])
    for i in range(3, 8):
        send(10, i, zero, zero)


def extend(dst, index, own, r16, r17, low):
    n = own.shape[0]
    dst[index, 0:n, :] = own
    dst[index, n : n + 1, :] = r16
    dst[index, n + 1 : n + 2, :] = r17
    dst[index, EXT - 1 : EXT, :] = low


def bulk_kernel(v, _, bulk):
    ny = v.shape[2]
    start, size = bulk_plan(v.shape[1], ny)
    bulk[0:8, :] = jnp.zeros((8, bulk.shape[1]), jnp.float32)
    bulk[size - 8 :, :] = jnp.zeros((8, bulk.shape[1]), jnp.float32)
    for (c, i), row in start.items():
        count = inner_rows(c, ny)
        bulk[row : row + count, :] = v[c, i, 2 : 2 + count, :]


def whole_flux(c, i, flux0, coeff, prev, lo_x, hi_x, lo_y, hi_y, rows):
    nx, ny = flux0.shape[1], flux0.shape[2]
    first, last = rows == 0, rows == ny - 1
    row = slice(i, i + 1)
    k = coeff[c, i]
    near = jnp.where(first, lo_y[c, row, :], 0.0) + jnp.where(last, hi_y[c, row, :], 0.0)
    if i == 0:
        near = near + lo_x[c]
    if i == nx - 1:
        near = near + hi_x[c]
    value = flux0[c, i] + share(k) * near
    if (c, i) not in ring_plan(nx, ny)[0]:
        inside = (rows > 1) & (rows < ny - (2 if c == 1 else 1))
        begin = bulk_plan(nx, ny)[0][c, i] - 2
        value = value + k * jnp.where(inside, prev[begin : begin + ny, :], 0.0)
    if c == 0 and i == nx - 1:
        value = value - k * hi_x[3]
    if c == 1:
        value = value - k * jnp.where(last, hi_y[3, row, :], 0.0)
    return value


def whole_layer(i, flows, before, s, total, out_rows, lo_y, right_x, scale_x, index, first):
    ny = s.shape[1]
    row = slice(i, i + 1)
    right = flows[0] + flows[1] - jnp.where(first, out_rows[0, row, :], below_y(flows[1]))
    right = right + flows[2] - below_z(flows[2]) - s[i]
    if before is not None:
        right = right - before
    scale = -DAMPING / (total[i] + jnp.where(first, lo_y[5, row, :], 0.0))
    extend(
        right_x, index, right,
        out_rows[2, row, :] - flows[1][ny - 1 : ny], out_rows[3, row, :], out_rows[1, row, :],
    )
    extend(scale_x, index, scale, out_rows[4, row, :], out_rows[6, row, :], out_rows[5, row, :])


def strip_kernel(
    flux0, coeff, s, total, lo_x, hi_x, got_odd, got_even, own,
    lo_y, hi_y, out_rows, send_odd, send_even, right_x, scale_x, side,
):
    nx, ny = s.shape[0], s.shape[1]
    even_x, even_y = is_even("gx"), is_even("gy")
    rows = row_id(s.shape[1:])
    first = rows == 0
    for layer in range(10):
        lo_y[layer], hi_y[layer] = pick(even_y, got_odd, got_even, slice(layer * nx, layer * nx + nx))
    lo_few, hi_few = pick(even_y, got_odd, got_even, slice(10 * nx, 10 * nx + 8))

    def along_x(x):
        return x - jnp.where(first_x, 0.0, pltpu.roll(x, 1, 0))

    first_x = row_id((nx, s.shape[2])) == 0
    edge = share(lo_y[4]) * own[0]
    push_y = share(lo_y[5]) * own[1] - lo_y[5] * own[6]
    push_z = share(lo_y[6]) * own[2]
    out_rows[0] = lo_y[3] + push_y
    out_rows[1] = lo_y[7] + along_x(edge) + push_y + push_z - below_z(push_z)
    out_rows[5] = lo_y[8]
    side_low = lo_few[0:1] + edge[nx - 1 :]
    edge = share(hi_y[4]) * own[3]
    push_y = share(hi_y[5]) * own[4]
    push_z = share(hi_y[6]) * own[5]
    out_rows[2] = hi_y[7] + along_x(edge) + push_y + push_z - below_z(push_z)
    out_rows[3] = hi_y[8] - push_y
    before = jnp.where(first_x, hi_few[2:3], pltpu.roll(hi_y[4], 1, 0))
    out_rows[4] = -DAMPING / (hi_y[4] + before + hi_y[5] + own[7] + hi_y[6] + below_z(hi_y[6]))
    out_rows[6] = hi_y[9]
    side_16, side_17 = hi_few[0:1] + edge[nx - 1 :], hi_few[1:2]

    right_x[...] = jnp.zeros_like(right_x)
    scale_x[...] = jnp.zeros_like(scale_x)
    side[...] = jnp.zeros_like(side)
    args = (flux0, coeff, None, lo_x, hi_x, lo_y, hi_y, rows)
    before = None
    for n, i in enumerate((0, 1, nx - 1)):
        if i == nx - 1:
            before = whole_flux(0, i - 1, *args)
        flows = [whole_flux(c, i, *args) for c in range(3)]
        whole_layer(i, flows, before, s, total, out_rows, lo_y, right_x, scale_x, n, first)
        before = flows[0]
    extend(side, 0, before, side_16, side_17, side_low)
    side[0, ny + 2 : ny + 3, :] = hi_y[4, nx - 1 : nx, :]
    scale_x[0, ny + 2 : ny + 3, :] = lo_y[5, 0:1, :]
    out_rows[7] = jnp.zeros(out_rows.shape[1:], jnp.float32)
    out_rows[7, 0:1, :] = side_low
    out_rows[7, 1:2, :] = side_16
    out_rows[7, 2:3, :] = side_17

    def send(layer, up, down):
        send_even[layer] = jnp.where(even_x, up, down)
        send_odd[layer] = jnp.where(even_x, down, up)

    send(0, right_x[2] * scale_x[2], right_x[1] * scale_x[1])
    send(1, side[0], right_x[0])
    send(2, jnp.zeros(side.shape[1:], jnp.float32), scale_x[0])


def sweep(low, mid, high, below_kx, kx, ky, kz, scale):
    gx = kx * (high - mid) - below_kx * (mid - low)
    gy = ky * (above_y(mid) - mid)
    gz = kz * (above_z(mid) - mid)
    applied = gx + gy - below_y(gy) + gz - below_z(gz)
    return 2.0 * mid - scale * applied


def own_kernel(
    flux0, coeff, prev, s, p, total, lo_x, hi_x, lo_y, hi_y, out_rows,
    flux, first_c, scale_x, side, kx, ky, kz, ends, wide_v, wide_p,
):
    nx, ny = s.shape[0], s.shape[1]
    rows = row_id(s.shape[1:])
    first = rows == 0
    args = (flux0, coeff, prev, lo_x, hi_x, lo_y, hi_y, rows)
    zero = jnp.zeros((1, s.shape[2]), jnp.float32)
    for ref in (first_c, scale_x, side, kx, ky, kz):
        ref[...] = jnp.zeros_like(ref)
    before = None
    for i in range(nx):
        row = slice(i, i + 1)
        flows = [whole_flux(c, i, *args) for c in range(3)]
        for c in range(3):
            flux[c, i] = flows[c]
        whole_layer(i, flows, before, s, total, out_rows, lo_y, first_c, scale_x, i, first)
        first_c[i] = first_c[i] * scale_x[i]
        before = flows[0]
        extend(kx, i, coeff[0, i], hi_y[4, row, :], zero, zero)
        extend(ky, i, coeff[1, i], hi_y[5, row, :], zero, lo_y[5, row, :])
        extend(kz, i, coeff[2, i], hi_y[6, row, :], zero, zero)
    extend(side, 0, before, out_rows[7, 1:2, :], out_rows[7, 2:3, :], out_rows[7, 0:1, :])
    now = None
    for i in range(2, nx - 1):
        after = sweep(first_c[i - 1], first_c[i], first_c[i + 1], kx[i - 1], kx[i], ky[i], kz[i], scale_x[i])
        wide_p[i - 2] = p[i] + after[:ny]
        wide_v[1, i - 2] = flux[1, i] - coeff[1, i] * (above_y(after) - after)[:ny]
        wide_v[2, i - 2] = flux[2, i] - coeff[2, i] * (above_z(after) - after)[:ny]
        if now is None:
            ends[0] = after
        else:
            wide_v[0, i - 3] = flux[0, i - 1] - coeff[0, i - 1] * (after - now)[:ny]
        now = after
    ends[1] = now


def last_kernel(
    flux, own_c, own_scale, side, own_kx, own_ky, own_kz, ends, p, lo_x, hi_x, got_odd, got_even, wide_v, wide_p,
    new_v, new_p, edge, low_v, low_p, top_v, top_p, top_x, sems,
):
    nx, ny = p.shape[0], p.shape[1]
    ready = [
        pltpu.make_async_copy(wide_v.at[0, pl.ds(0, nx - 4)], new_v.at[0, pl.ds(2, nx - 4)], sems.at[5]),
        pltpu.make_async_copy(wide_v.at[1], new_v.at[1, pl.ds(2, nx - 3)], sems.at[6]),
        pltpu.make_async_copy(wide_v.at[2], new_v.at[2, pl.ds(2, nx - 3)], sems.at[7]),
        pltpu.make_async_copy(wide_p, new_p.at[pl.ds(2, nx - 3)], sems.at[8]),
    ]
    for copy in ready:
        copy.start()
    even_x = is_even("gx")
    lo0, hi0 = pick(even_x, got_odd, got_even, 0)
    lo1, hi1 = pick(even_x, got_odd, got_even, 1)
    _, hi2 = pick(even_x, got_odd, got_even, 2)
    edge[...] = jnp.zeros_like(edge)
    edge[0, 0:ny, :] = lo_x[4]
    edge[0, ny : ny + 1, :] = lo1[ny + 2 : ny + 3, :]
    edge[1, 0:ny, :] = hi_x[4]
    edge[2, 0:ny, :] = hi_x[5]
    edge[2, EXT - 1 : EXT, :] = hi2[ny + 2 : ny + 3, :]
    edge[3, 0:ny, :] = hi_x[6]
    zeroth = own_c[0] - lo1 * own_scale[0]
    beyond = (hi1 - side[0]) * hi2
    at = lambda i: (own_kx[i], own_ky[i], own_kz[i], own_scale[i])
    second = {
        0: sweep(lo0, zeroth, own_c[1], edge[0], *at(0)),
        1: sweep(zeroth, own_c[1], own_c[2], own_kx[0], *at(1)),
        2: ends[0],
        nx - 2: ends[1],
        nx - 1: sweep(own_c[nx - 2], own_c[nx - 1], beyond, own_kx[nx - 2], *at(nx - 1)),
        nx: sweep(own_c[nx - 1], beyond, hi0, own_kx[nx - 1], edge[1], edge[2], edge[3], hi2),
    }

    def step_x(i):
        return flux[0, i] - own_kx[i, :ny] * (second[i + 1] - second[i])[:ny]

    def step_y(i):
        return flux[1, i] - own_ky[i, :ny] * (above_y(second[i]) - second[i])[:ny]

    def step_z(i):
        return flux[2, i] - own_kz[i, :ny] * (above_z(second[i]) - second[i])[:ny]

    for n, i in enumerate((0, 1)):
        low_v[0, n], low_v[1, n], low_v[2, n] = step_x(i), step_y(i), step_z(i)
        low_p[n] = p[i] + second[i][:ny]
    top_v[0, 0], top_v[1, 0], top_v[2, 0] = step_x(nx - 1), step_y(nx - 1), step_z(nx - 1)
    top_p[0] = p[nx - 1] + second[nx - 1][:ny]
    top_x[0] = step_x(nx - 2)
    copies = [
        pltpu.make_async_copy(low_v, new_v.at[:, pl.ds(0, 2)], sems.at[0]),
        pltpu.make_async_copy(top_v, new_v.at[:, pl.ds(nx - 1, 1)], sems.at[1]),
        pltpu.make_async_copy(top_x, new_v.at[0, pl.ds(nx - 2, 1)], sems.at[2]),
        pltpu.make_async_copy(low_p, new_p.at[pl.ds(0, 2)], sems.at[3]),
        pltpu.make_async_copy(top_p, new_p.at[pl.ds(nx - 1, 1)], sems.at[4]),
    ]
    for copy in copies:
        copy.start()
    for copy in ready + copies:
        copy.wait()


VM = pl.BlockSpec(memory_space=pltpu.VMEM)


ANY = pl.BlockSpec(memory_space=pl.ANY)


def call(kernel, args, outs, scratch=(), flops=1000, far=0):
    shapes = [jax.ShapeDtypeStruct(s, jnp.float32) for s in outs]
    size = sum(4 * a.size for a in args) + sum(4 * s.size for s in shapes)
    return pl.pallas_call(
        kernel,
        out_shape=shapes,
        in_specs=[VM] * len(args),
        out_specs=[VM] * (len(shapes) - far) + [ANY] * far,
        scratch_shapes=[pltpu.VMEM(s, jnp.float32) for s in scratch] + [pltpu.SemaphoreType.DMA((9,))] * (far > 0),
        compiler_params=pltpu.CompilerParams(vmem_limit_bytes=40 * 2**20),
        cost_estimate=pl.CostEstimate(flops=flops, bytes_accessed=size, transcendentals=0),
    )(*args)


def body(velocity, pressure, forcing, source, viscosity):
    v, p, f, s = velocity[:, 0], pressure[0], forcing[:, 0], source[0]
    nx, ny, nz = p.shape
    steps = lax.axis_size("ta")
    ahead = [(i, i + 1) for i in range(steps - 1)]
    (ring,) = call(ring_kernel, (v,), ((ring_plan(nx, ny)[3], ny, nz),), flops=20_000_000_000)
    face_odd, face_even = call(face_kernel, (v, p, viscosity), ((7, ny, nz), (7, ny, nz)), flops=20_000_000_000)
    odd_x, even_x = swap_odd(face_odd, "gx"), swap_even(face_even, "gx")
    ring = lax.ppermute(ring, "ta", ahead)
    flux0, coeff = call(local_kernel, (v, p, f, viscosity, ring), (v.shape,) * 2)
    lo_x, hi_x, total, send_odd, send_even, own = call(
        edge_kernel,
        (flux0, coeff, v, p, s, odd_x, even_x),
        ((7, ny, nz), (7, ny, nz), p.shape, (10 * nx + 8, nz), (10 * nx + 8, nz), (8, nx, nz)),
    )
    (bulk,) = call(bulk_kernel, (v, total), ((bulk_plan(nx, ny)[1], nz),))
    prev = lax.ppermute(bulk, "ta", ahead)
    odd_y, even_y = swap_odd(send_odd, "gy"), swap_even(send_even, "gy")
    lo_y, hi_y, out_rows, send_odd, send_even = call(
        strip_kernel,
        (flux0, coeff, s, total, lo_x, hi_x, odd_y, even_y, own),
        ((10, nx, nz), (10, nx, nz), (8, nx, nz), (3, EXT, nz), (3, EXT, nz)),
        ((3, EXT, nz), (3, EXT, nz), (1, EXT, nz)),
        flops=20_000_000_000,
    )
    odd_x, even_x = swap_odd(send_odd, "gx"), swap_even(send_even, "gx")
    flux, first_c, scale, side, kx, ky, kz, ends, wide_v, wide_p = call(
        own_kernel,
        (flux0, coeff, prev, s, p, total, lo_x, hi_x, lo_y, hi_y, out_rows),
        (v.shape, (nx, EXT, nz), (nx, EXT, nz), (1, EXT, nz))
        + ((nx, EXT, nz),) * 3
        + ((2, EXT, nz), (3, nx - 3, ny, nz), (nx - 3, ny, nz)),
    )
    new_v, new_p = call(
        last_kernel,
        (flux, first_c, scale, side, kx, ky, kz, ends, p, lo_x, hi_x, odd_x, even_x, wide_v, wide_p),
        (v.shape, p.shape),
        ((4, EXT, nz), (3, 2, ny, nz), (2, ny, nz), (3, 1, ny, nz), (1, ny, nz), (1, ny, nz)),
        far=2,
    )
    return new_v[:, None], new_p[None]


def solution(mesh):
    placed = (
        P(None, "ta", "gx", "gy", None),
        P("ta", "gx", "gy", None),
        P(None, "ta", "gx", "gy", None),
        P("ta", "gx", "gy", None),
        P(None, "gx", "gy", None),
    )
    return jax.shard_map(
        body,
        mesh=mesh,
        in_specs=placed,
        out_specs=(P(None, "ta", "gx", "gy", None), P("ta", "gx", "gy", None)),
        check_vma=False,
    )
```

```python
import jax
import jax.numpy as jnp
from jax import lax
from jax.experimental import pallas as pl
from jax.experimental.pallas import tpu as pltpu
from jax.sharding import PartitionSpec as P

RELAX = 1.5
DAMPING = 0.8
MORE = 2
EXT = 24


def odd_pairs(n):
    return [p for i in range(1, n, 2) for p in ((i, (i + 1) % n), ((i + 1) % n, i))]


def even_pairs(n):
    return [p for i in range(0, n, 2) for p in ((i, i + 1), (i + 1, i))]


def swap_odd(x, axis):
    return lax.ppermute(x, axis, odd_pairs(lax.axis_size(axis)))


def swap_even(x, axis):
    return lax.ppermute(x, axis, even_pairs(lax.axis_size(axis)))


def is_even(axis):
    return lax.rem(lax.axis_index(axis), 2) == 0


def above_z(x):
    return pltpu.roll(x, x.shape[1] - 1, 1)


def below_z(x):
    return pltpu.roll(x, 1, 1)


def above_y(x):
    return pltpu.roll(x, x.shape[0] - 1, 0)


def below_y(x):
    return pltpu.roll(x, 1, 0)


def row_id(shape):
    return lax.broadcasted_iota(jnp.int32, shape, 0)


def coeff_of(visc):
    return 1.0 / (RELAX * (1.0 + 6.0 * visc))


def ring_plan(nx, ny):
    layers = [(c, i) for c in range(3) for i in (*range(2 + MORE), nx - 1)] + [(0, nx - 2)]
    whole = {key: tile for tile, key in enumerate(layers)}
    lines = [(0, 1, ny - 1), (0, 1, ny - 2, ny - 1), (0, 1, ny - 1)]
    single = {}
    for c in range(3):
        for i in range(nx):
            if (c, i) not in whole:
                for j in lines[c]:
                    tile, row = divmod(len(single), ny)
                    single[c, i, j] = (len(whole) + tile, row)
    return whole, single, lines, len(whole) + -(-len(single) // ny)


def bulk_plan(nx, ny):
    whole = ring_plan(nx, ny)[0]
    start, used = {}, 2
    for c in range(3):
        for i in range(nx):
            if (c, i) not in whole:
                start[c, i] = used
                used += inner_rows(c, ny)
    return start, -(-(used + 4) // 8) * 8


def inner_rows(c, ny):
    return ny - (4 if c == 1 else 3)


def share(c):
    return (1.0 / RELAX - c) * (1.0 / 6.0)


def pick(even, odd_got, even_got, index):
    a, b = odd_got[index], even_got[index]
    return jnp.where(even, a, b), jnp.where(even, b, a)


def ring_kernel(v, ring):
    nx, ny = v.shape[1], v.shape[2]
    whole, single, _, tiles = ring_plan(nx, ny)
    ring[tiles - 1] = jnp.zeros(ring.shape[1:], jnp.float32)
    for (c, i), tile in whole.items():
        ring[tile] = v[c, i]
    for (c, i, j), (tile, row) in single.items():
        ring[tile, row : row + 1, :] = v[c, i, j : j + 1, :]


def face_kernel(v, p, visc, send_odd, send_even):
    nx = v.shape[1]
    even_x = is_even("gx")

    def send(layer, up, down):
        send_even[layer] = jnp.where(even_x, up, down)
        send_odd[layer] = jnp.where(even_x, down, up)

    for c in range(3):
        send(c, v[c, nx - 1], v[c, 0])
        send(4 + c, coeff_of(visc[c, nx - 1]), coeff_of(visc[c, 0]))
    send(3, jnp.zeros(p.shape[1:], jnp.float32), p[0])


def local_kernel(v, p, f, visc, ring, flux, coeff):
    nx, ny = p.shape[0], p.shape[1]
    rows = row_id(p.shape[1:])
    first, last = rows == 0, rows == ny - 1
    whole, single, lines, _ = ring_plan(nx, ny)
    for i in range(nx):
        pressure = p[i]
        slope_x = (p[i + 1] if i + 1 < nx else jnp.zeros_like(pressure)) - pressure
        slope_y = jnp.where(last, 0.0, above_y(pressure)) - pressure
        slope_z = above_z(pressure) - pressure
        for c, slope in enumerate((slope_x, slope_y, slope_z)):
            nu = visc[c, i]
            k = coeff_of(nu)
            flow = v[c, i]
            near = above_z(flow) + below_z(flow)
            near = near + jnp.where(last, 0.0, above_y(flow)) + jnp.where(first, 0.0, below_y(flow))
            if i > 0:
                near = near + v[c, i - 1]
            if i + 1 < nx:
                near = near + v[c, i + 1]
            coeff[c, i] = k
            if (c, i) in whole:
                prev = ring[whole[c, i]]
            else:
                prev = jnp.zeros(p.shape[1:], jnp.float32)
                for j in lines[c]:
                    tile, row = single[c, i, j]
                    prev = jnp.where(rows == j, ring[tile, row : row + 1, :], prev)
            flux[c, i] = k * (f[c, i] + prev + nu * near - slope) + flow * (1.0 - 1.0 / RELAX)


def edge_kernel(flux0, coeff, v, p, s, got_odd, got_even, lo_x, hi_x, total, send_odd, send_even, own):
    nx, ny = s.shape[0], s.shape[1]
    shape = s.shape[1:]
    rows = row_id(shape)
    first = rows == 0
    even_y = is_even("gy")
    zero = jnp.zeros((1, shape[1]), jnp.float32)
    top, low, near = slice(ny - 1, ny), slice(0, 1), slice(1, 2)
    for layer in range(7):
        lo_x[layer], hi_x[layer] = pick(is_even("gx"), got_odd, got_even, layer)

    def send(layer, i, up, down):
        row = layer * nx + i
        send_even[row : row + 1, :] = jnp.where(even_y, up, down)
        send_odd[row : row + 1, :] = jnp.where(even_y, down, up)

    before = None
    for i in range(nx):
        row = slice(i, i + 1)
        flows = []
        for c in range(3):
            k = coeff[c, i]
            value = flux0[c, i]
            if i == 0:
                value = value + share(k) * lo_x[c]
            if i == nx - 1:
                value = value + share(k) * hi_x[c]
                if c == 0:
                    value = value - k * hi_x[3]
            flows.append(value)
        right = flows[0] + flows[1] - jnp.where(first, 0.0, below_y(flows[1])) + flows[2] - below_z(flows[2])
        right = right - s[i]
        kx, ky, kz = coeff[0, i], coeff[1, i], coeff[2, i]
        tot = kx + ky + jnp.where(first, 0.0, below_y(ky)) + kz + below_z(kz)
        if i > 0:
            right = right - before
            tot = tot + coeff[0, i - 1]
        else:
            tot = tot + lo_x[4]
        before = flows[0]
        total[i] = tot
        over = -DAMPING / tot
        for c in range(3):
            send(c, i, v[c, i, top, :], v[c, i, low, :])
            send(4 + c, i, coeff[c, i, top, :], coeff[c, i, low, :])
            own[c, row, :] = v[c, i, low, :]
            own[3 + c, row, :] = v[c, i, top, :]
        own[6, row, :] = p[i, low, :]
        own[7, row, :] = coeff[1, i, top, :]
        send(3, i, flows[1][top], p[i, low, :])
        send(7, i, right[top], right[low])
        send(8, i, over[top], right[near])
        send(9, i, zero, over[near])
    send(10, 0, before[top], before[low])
    send(10, 1, zero, before[near])
    send(10, 2, zero, lo_x[4, low, :])
    for i in range(3, 8):
        send(10, i, zero, zero)


def extend(dst, index, own, r16, r17, low):
    n = own.shape[0]
    dst[index, 0:n, :] = own
    dst[index, n : n + 1, :] = r16
    dst[index, n + 1 : n + 2, :] = r17
    dst[index, EXT - 1 : EXT, :] = low


def bulk_kernel(v, _, bulk):
    ny = v.shape[2]
    start, size = bulk_plan(v.shape[1], ny)
    bulk[0:8, :] = jnp.zeros((8, bulk.shape[1]), jnp.float32)
    bulk[size - 8 :, :] = jnp.zeros((8, bulk.shape[1]), jnp.float32)
    for (c, i), row in start.items():
        count = inner_rows(c, ny)
        bulk[row : row + count, :] = v[c, i, 2 : 2 + count, :]


def whole_flux(c, i, flux0, coeff, prev, lo_x, hi_x, lo_y, hi_y, rows):
    nx, ny = flux0.shape[1], flux0.shape[2]
    first, last = rows == 0, rows == ny - 1
    row = slice(i, i + 1)
    k = coeff[c, i]
    near = jnp.where(first, lo_y[c, row, :], 0.0) + jnp.where(last, hi_y[c, row, :], 0.0)
    if i == 0:
        near = near + lo_x[c]
    if i == nx - 1:
        near = near + hi_x[c]
    value = flux0[c, i] + share(k) * near
    if (c, i) not in ring_plan(nx, ny)[0]:
        inside = (rows > 1) & (rows < ny - (2 if c == 1 else 1))
        begin = bulk_plan(nx, ny)[0][c, i] - 2
        value = value + k * jnp.where(inside, prev[begin : begin + ny, :], 0.0)
    if c == 0 and i == nx - 1:
        value = value - k * hi_x[3]
    if c == 1:
        value = value - k * jnp.where(last, hi_y[3, row, :], 0.0)
    return value


def whole_layer(i, flows, before, s, total, out_rows, lo_y, right_x, scale_x, index, first):
    ny = s.shape[1]
    row = slice(i, i + 1)
    right = flows[0] + flows[1] - jnp.where(first, out_rows[0, row, :], below_y(flows[1]))
    right = right + flows[2] - below_z(flows[2]) - s[i]
    if before is not None:
        right = right - before
    scale = -DAMPING / (total[i] + jnp.where(first, lo_y[5, row, :], 0.0))
    extend(
        right_x, index, right,
        out_rows[2, row, :] - flows[1][ny - 1 : ny], out_rows[3, row, :], out_rows[1, row, :],
    )
    extend(scale_x, index, scale, out_rows[4, row, :], out_rows[6, row, :], out_rows[5, row, :])


def strip_kernel(
    flux0, coeff, s, total, lo_x, hi_x, got_odd, got_even, own,
    lo_y, hi_y, out_rows, send_odd, send_even, right_x, scale_x, side,
):
    nx, ny = s.shape[0], s.shape[1]
    even_x, even_y = is_even("gx"), is_even("gy")
    rows = row_id(s.shape[1:])
    first = rows == 0
    for layer in range(10):
        lo_y[layer], hi_y[layer] = pick(even_y, got_odd, got_even, slice(layer * nx, layer * nx + nx))
    lo_few, hi_few = pick(even_y, got_odd, got_even, slice(10 * nx, 10 * nx + 8))

    def along_x(x):
        return x - jnp.where(first_x, 0.0, pltpu.roll(x, 1, 0))

    first_x = row_id((nx, s.shape[2])) == 0
    edge = share(lo_y[4]) * own[0]
    push_y = share(lo_y[5]) * own[1] - lo_y[5] * own[6]
    push_z = share(lo_y[6]) * own[2]
    out_rows[0] = lo_y[3] + push_y
    out_rows[1] = lo_y[7] + along_x(edge) + push_y + push_z - below_z(push_z)
    out_rows[5] = lo_y[8]
    side_low = lo_few[0:1] + edge[nx - 1 :]
    edge = share(hi_y[4]) * own[3]
    push_y = share(hi_y[5]) * own[4]
    push_z = share(hi_y[6]) * own[5]
    out_rows[2] = hi_y[7] + along_x(edge) + push_y + push_z - below_z(push_z)
    out_rows[3] = hi_y[8] - push_y
    before = jnp.where(first_x, hi_few[2:3], pltpu.roll(hi_y[4], 1, 0))
    out_rows[4] = -DAMPING / (hi_y[4] + before + hi_y[5] + own[7] + hi_y[6] + below_z(hi_y[6]))
    out_rows[6] = hi_y[9]
    side_16, side_17 = hi_few[0:1] + edge[nx - 1 :], hi_few[1:2]

    for ref in (right_x, scale_x, side):
        ref[:, ny:, :] = jnp.zeros((ref.shape[0], EXT - ny, ref.shape[2]), jnp.float32)
    args = (flux0, coeff, None, lo_x, hi_x, lo_y, hi_y, rows)
    before = None
    for n, i in enumerate((0, 1, nx - 1)):
        if i == nx - 1:
            before = whole_flux(0, i - 1, *args)
        flows = [whole_flux(c, i, *args) for c in range(3)]
        whole_layer(i, flows, before, s, total, out_rows, lo_y, right_x, scale_x, n, first)
        before = flows[0]
    extend(side, 0, before, side_16, side_17, side_low)
    side[0, ny + 2 : ny + 3, :] = hi_y[4, nx - 1 : nx, :]
    scale_x[0, ny + 2 : ny + 3, :] = lo_y[5, 0:1, :]
    out_rows[7] = jnp.zeros(out_rows.shape[1:], jnp.float32)
    out_rows[7, 0:1, :] = side_low
    out_rows[7, 1:2, :] = side_16
    out_rows[7, 2:3, :] = side_17

    def send(layer, up, down):
        send_even[layer] = jnp.where(even_x, up, down)
        send_odd[layer] = jnp.where(even_x, down, up)

    send(0, right_x[2] * scale_x[2], right_x[1] * scale_x[1])
    send(1, side[0], right_x[0])
    send(2, jnp.zeros(side.shape[1:], jnp.float32), scale_x[0])


def sweep(low, mid, high, below_kx, kx, ky, kz, scale):
    gx = kx * (high - mid) - below_kx * (mid - low)
    gy = ky * (above_y(mid) - mid)
    gz = kz * (above_z(mid) - mid)
    applied = gx + gy - below_y(gy) + gz - below_z(gz)
    return 2.0 * mid - scale * applied


def own_kernel(
    flux0, coeff, prev, s, p, total, lo_x, hi_x, lo_y, hi_y, out_rows,
    flux, first_c, scale_x, side, kx, ky, kz, ends, wide_v, wide_p,
):
    nx, ny = s.shape[0], s.shape[1]
    rows = row_id(s.shape[1:])
    first = rows == 0
    args = (flux0, coeff, prev, lo_x, hi_x, lo_y, hi_y, rows)
    zero = jnp.zeros((1, s.shape[2]), jnp.float32)
    for ref in (first_c, scale_x, side, kx, ky, kz):
        ref[:, ny:, :] = jnp.zeros((ref.shape[0], EXT - ny, ref.shape[2]), jnp.float32)
    before = None
    for i in range(nx):
        row = slice(i, i + 1)
        flows = [whole_flux(c, i, *args) for c in range(3)]
        for c in range(3):
            flux[c, i] = flows[c]
        whole_layer(i, flows, before, s, total, out_rows, lo_y, first_c, scale_x, i, first)
        first_c[i] = first_c[i] * scale_x[i]
        before = flows[0]
        extend(kx, i, coeff[0, i], hi_y[4, row, :], zero, zero)
        extend(ky, i, coeff[1, i], hi_y[5, row, :], zero, lo_y[5, row, :])
        extend(kz, i, coeff[2, i], hi_y[6, row, :], zero, zero)
    extend(side, 0, before, out_rows[7, 1:2, :], out_rows[7, 2:3, :], out_rows[7, 0:1, :])
    now = None
    for i in range(2, nx - 1):
        after = sweep(first_c[i - 1], first_c[i], first_c[i + 1], kx[i - 1], kx[i], ky[i], kz[i], scale_x[i])
        wide_p[i - 2] = p[i] + after[:ny]
        wide_v[1, i - 2] = flux[1, i] - coeff[1, i] * (above_y(after) - after)[:ny]
        wide_v[2, i - 2] = flux[2, i] - coeff[2, i] * (above_z(after) - after)[:ny]
        if now is None:
            ends[0] = after
        else:
            wide_v[0, i - 3] = flux[0, i - 1] - coeff[0, i - 1] * (after - now)[:ny]
        now = after
    ends[1] = now


def last_kernel(
    flux, own_c, own_scale, side, own_kx, own_ky, own_kz, ends, p, lo_x, hi_x, got_odd, got_even, wide_v, wide_p,
    new_v, new_p, edge, low_v, low_p, top_v, top_p, top_x, sems,
):
    nx, ny = p.shape[0], p.shape[1]
    ready = [
        pltpu.make_async_copy(wide_v.at[0, pl.ds(0, nx - 4)], new_v.at[0, pl.ds(2, nx - 4)], sems.at[5]),
        pltpu.make_async_copy(wide_v.at[1], new_v.at[1, pl.ds(2, nx - 3)], sems.at[6]),
        pltpu.make_async_copy(wide_v.at[2], new_v.at[2, pl.ds(2, nx - 3)], sems.at[7]),
        pltpu.make_async_copy(wide_p, new_p.at[pl.ds(2, nx - 3)], sems.at[8]),
    ]
    for copy in ready:
        copy.start()
    even_x = is_even("gx")
    lo0, hi0 = pick(even_x, got_odd, got_even, 0)
    lo1, hi1 = pick(even_x, got_odd, got_even, 1)
    _, hi2 = pick(even_x, got_odd, got_even, 2)
    edge[...] = jnp.zeros_like(edge)
    edge[0, 0:ny, :] = lo_x[4]
    edge[0, ny : ny + 1, :] = lo1[ny + 2 : ny + 3, :]
    edge[1, 0:ny, :] = hi_x[4]
    edge[2, 0:ny, :] = hi_x[5]
    edge[2, EXT - 1 : EXT, :] = hi2[ny + 2 : ny + 3, :]
    edge[3, 0:ny, :] = hi_x[6]
    zeroth = own_c[0] - lo1 * own_scale[0]
    beyond = (hi1 - side[0]) * hi2
    at = lambda i: (own_kx[i], own_ky[i], own_kz[i], own_scale[i])
    second = {
        0: sweep(lo0, zeroth, own_c[1], edge[0], *at(0)),
        1: sweep(zeroth, own_c[1], own_c[2], own_kx[0], *at(1)),
        2: ends[0],
        nx - 2: ends[1],
        nx - 1: sweep(own_c[nx - 2], own_c[nx - 1], beyond, own_kx[nx - 2], *at(nx - 1)),
        nx: sweep(own_c[nx - 1], beyond, hi0, own_kx[nx - 1], edge[1], edge[2], edge[3], hi2),
    }

    def step_x(i):
        return flux[0, i] - own_kx[i, :ny] * (second[i + 1] - second[i])[:ny]

    def step_y(i):
        return flux[1, i] - own_ky[i, :ny] * (above_y(second[i]) - second[i])[:ny]

    def step_z(i):
        return flux[2, i] - own_kz[i, :ny] * (above_z(second[i]) - second[i])[:ny]

    for n, i in enumerate((0, 1)):
        low_v[0, n], low_v[1, n], low_v[2, n] = step_x(i), step_y(i), step_z(i)
        low_p[n] = p[i] + second[i][:ny]
    low = [
        pltpu.make_async_copy(low_v, new_v.at[:, pl.ds(0, 2)], sems.at[0]),
        pltpu.make_async_copy(low_p, new_p.at[pl.ds(0, 2)], sems.at[1]),
    ]
    for copy in low:
        copy.start()
    top_v[0, 0], top_v[1, 0], top_v[2, 0] = step_x(nx - 1), step_y(nx - 1), step_z(nx - 1)
    top_p[0] = p[nx - 1] + second[nx - 1][:ny]
    top_x[0] = step_x(nx - 2)
    top = [
        pltpu.make_async_copy(top_v, new_v.at[:, pl.ds(nx - 1, 1)], sems.at[2]),
        pltpu.make_async_copy(top_x, new_v.at[0, pl.ds(nx - 2, 1)], sems.at[3]),
        pltpu.make_async_copy(top_p, new_p.at[pl.ds(nx - 1, 1)], sems.at[4]),
    ]
    for copy in top:
        copy.start()
    for copy in ready + low + top:
        copy.wait()


VM = pl.BlockSpec(memory_space=pltpu.VMEM)


ANY = pl.BlockSpec(memory_space=pl.ANY)


def call(kernel, args, outs, scratch=(), flops=1000, far=0):
    shapes = [jax.ShapeDtypeStruct(s, jnp.float32) for s in outs]
    size = sum(4 * a.size for a in args) + sum(4 * s.size for s in shapes)
    return pl.pallas_call(
        kernel,
        out_shape=shapes,
        in_specs=[VM] * len(args),
        out_specs=[VM] * (len(shapes) - far) + [ANY] * far,
        scratch_shapes=[pltpu.VMEM(s, jnp.float32) for s in scratch] + [pltpu.SemaphoreType.DMA((9,))] * (far > 0),
        compiler_params=pltpu.CompilerParams(vmem_limit_bytes=40 * 2**20),
        cost_estimate=pl.CostEstimate(flops=flops, bytes_accessed=size, transcendentals=0),
    )(*args)


def body(velocity, pressure, forcing, source, viscosity):
    v, p, f, s = velocity[:, 0], pressure[0], forcing[:, 0], source[0]
    nx, ny, nz = p.shape
    steps = lax.axis_size("ta")
    ahead = [(i, i + 1) for i in range(steps - 1)]
    (ring,) = call(ring_kernel, (v,), ((ring_plan(nx, ny)[3], ny, nz),), flops=20_000_000_000)
    face_odd, face_even = call(face_kernel, (v, p, viscosity), ((7, ny, nz), (7, ny, nz)), flops=20_000_000_000)
    odd_x, even_x = swap_odd(face_odd, "gx"), swap_even(face_even, "gx")
    ring = lax.ppermute(ring, "ta", ahead)
    flux0, coeff = call(local_kernel, (v, p, f, viscosity, ring), (v.shape,) * 2)
    lo_x, hi_x, total, send_odd, send_even, own = call(
        edge_kernel,
        (flux0, coeff, v, p, s, odd_x, even_x),
        ((7, ny, nz), (7, ny, nz), p.shape, (10 * nx + 8, nz), (10 * nx + 8, nz), (8, nx, nz)),
    )
    (bulk,) = call(bulk_kernel, (v, total), ((bulk_plan(nx, ny)[1], nz),))
    prev = lax.ppermute(bulk, "ta", ahead)
    odd_y, even_y = swap_odd(send_odd, "gy"), swap_even(send_even, "gy")
    lo_y, hi_y, out_rows, send_odd, send_even = call(
        strip_kernel,
        (flux0, coeff, s, total, lo_x, hi_x, odd_y, even_y, own),
        ((10, nx, nz), (10, nx, nz), (8, nx, nz), (3, EXT, nz), (3, EXT, nz)),
        ((3, EXT, nz), (3, EXT, nz), (1, EXT, nz)),
        flops=20_000_000_000,
    )
    odd_x, even_x = swap_odd(send_odd, "gx"), swap_even(send_even, "gx")
    flux, first_c, scale, side, kx, ky, kz, ends, wide_v, wide_p = call(
        own_kernel,
        (flux0, coeff, prev, s, p, total, lo_x, hi_x, lo_y, hi_y, out_rows),
        (v.shape, (nx, EXT, nz), (nx, EXT, nz), (1, EXT, nz))
        + ((nx, EXT, nz),) * 3
        + ((2, EXT, nz), (3, nx - 3, ny, nz), (nx - 3, ny, nz)),
    )
    new_v, new_p = call(
        last_kernel,
        (flux, first_c, scale, side, kx, ky, kz, ends, p, lo_x, hi_x, odd_x, even_x, wide_v, wide_p),
        (v.shape, p.shape),
        ((4, EXT, nz), (3, 2, ny, nz), (2, ny, nz), (3, 1, ny, nz), (1, ny, nz), (1, ny, nz)),
        far=2,
    )
    return new_v[:, None], new_p[None]


def solution(mesh):
    placed = (
        P(None, "ta", "gx", "gy", None),
        P("ta", "gx", "gy", None),
        P(None, "ta", "gx", "gy", None),
        P("ta", "gx", "gy", None),
        P(None, "gx", "gy", None),
    )
    return jax.shard_map(
        body,
        mesh=mesh,
        in_specs=placed,
        out_specs=(P(None, "ta", "gx", "gy", None), P("ta", "gx", "gy", None)),
        check_vma=False,
    )
```
